32 devices in a mesh: shard: 8 (over z, x), rep: 4 (over y, core).
Axes of the slice: x: 2, y: 2, z: 4, core: 2. Of those that a mesh axis runs over, the one named last changes fastest.
Arguments:
- tokens: bfloat16 [4, 4096, 1024], P('rep', 'shard'), may hold values from -15 to 15
- cotangent: bfloat16 [4, 4096, 1024], P('rep', 'shard'), may hold values from -6 to 6
- in_weight: bfloat16 [1024, 3072], P('shard'), may hold values from -0.1875 to 0.1875
- out_weight: bfloat16 [1024, 1024], P('shard'), may hold values from -0.1875 to 0.1875
- gate_weight: bfloat16 [1024, 4608], P('shard'), may hold values from -0.1875 to 0.1875
- up_weight: bfloat16 [1024, 4608], P('shard'), may hold values from -0.1875 to 0.1875
- down_weight: bfloat16 [4608, 1024], P('shard'), may hold values from -0.09375 to 0.09375
- mix_gain: bfloat16 [1024], P('shard'), may hold values from 0.5 to 1.5
- ffn_gain: bfloat16 [1024], P('shard'), may hold values from 0.5 to 1.5
- conv_taps: bfloat16 [3, 1024], P(None, 'shard'), may hold values from -3 to 3
Outputs:
- output: bfloat16 [4, 4096, 1024], P('rep', 'shard')
- grad_tokens: bfloat16 [4, 4096, 1024], P('rep', 'shard')
- grad_in: float32 [1024, 3072], P('shard')
- grad_out: float32 [1024, 1024], P('shard')
- grad_gate: float32 [1024, 4608], P('shard')
- grad_up: float32 [1024, 4608], P('shard')
- grad_down: float32 [4608, 1024], P('shard')
- grad_mix_gain: float32 [1024], P('shard')
- grad_ffn_gain: float32 [1024], P('shard')
- grad_taps: float32 [3, 1024], P(None, 'shard')
The draws below stay inside these ranges and needn't reach their ends.
All inputs are finite; a program needn't handle non-finite values.
Results may differ from the reference program's by a relative error of at most 0.0097.
Values may be sent and summed in bfloat16 or wider, within the bound.
No kernel may reach another device: no remote copies, remote signals or barrier semaphores. Data moves between devices by JAX's collectives and lax.ppermute only.
A program may use at most 192 MiB of HBM per device.

```python
import math
import jax
import jax.numpy as jnp
from jax import lax

D = 1024
FF = 4608
TAPS = 3
LENGTH = 4096
SEQS = 4


def draw_tokens(key, part):
    key = jax.random.fold_in(key, 11)
    key_rows, key_base = jax.random.split(key, 2)
    scales = jnp.exp(jax.random.uniform(key_rows, (SEQS, LENGTH, 1), jnp.float32, math.log(0.3), math.log(3.0)))
    base = jnp.clip(jax.random.normal(key_base, (SEQS, LENGTH, D), jnp.float32), -5.0, 5.0)
    return (scales * base).astype(jnp.bfloat16)


def level_of(rng, dims, cuts, low, top_value):
    loudness = 1.0
    for axis_at, parts in cuts:
        draws = jax.random.uniform(jax.random.fold_in(jax.random.fold_in(rng, 6), axis_at), (parts,), jnp.float32, low / len(cuts), top_value / len(cuts))
        loudness = loudness * jnp.repeat(jnp.exp(draws), dims[axis_at] // parts).reshape((-1,) + (1,) * (len(dims) - 1 - axis_at))
    return loudness


def centred(rng, shape, scale, limit, cuts=(), kind=jnp.bfloat16):
    level = level_of(rng, shape, cuts, -0.22, 0.18) if cuts else 1.0
    entries = jax.random.normal(rng, shape, jnp.float32) * scale * level
    return jnp.minimum(jnp.maximum(entries, -limit), limit).astype(kind)


def setup_inputs(seed: int = 0) -> dict:
    arg_keys = jax.random.split(jax.random.key(seed), 11)
    return {
        "tokens": draw_tokens(jax.random.fold_in(arg_keys[10], 71), 0),
        "cotangent": centred(arg_keys[1], (SEQS, LENGTH, D), 1.0, 6.0, ((0, 4), (1, 8))),
        "in_weight": centred(arg_keys[2], (D, 3 * D), D ** -0.5, 0.1875, ((0, 8),)),
        "out_weight": centred(arg_keys[3], (D, D), D ** -0.5, 0.1875, ((0, 8),)),
        "gate_weight": centred(arg_keys[4], (D, FF), D ** -0.5, 0.1875, ((0, 8),)),
        "up_weight": centred(arg_keys[5], (D, FF), D ** -0.5, 0.1875, ((0, 8),)),
        "down_weight": centred(arg_keys[6], (FF, D), FF ** -0.5, 0.09375, ((0, 8),)),
        "mix_gain": jnp.clip(1.0 + 0.1 * jax.random.normal(arg_keys[7], (D,), jnp.float32), 0.5, 1.5).astype(jnp.bfloat16),
        "ffn_gain": jnp.clip(1.0 + 0.1 * jax.random.normal(arg_keys[8], (D,), jnp.float32), 0.5, 1.5).astype(jnp.bfloat16),
        "conv_taps": centred(arg_keys[9], (TAPS, D), 0.6, 3.0, ((1, 8),)),
    }


epsilon = 1e-05

@jax.custom_vjp
def low(v):
    return lax.optimization_barrier(v.astype(jnp.bfloat16)).astype(jnp.float32)

@jax.custom_vjp
def low_back(v):
    return v

def low_keep(v):
    return (low(v), None)

def low_pass(kept, grad):
    return (grad,)

def back_keep(v):
    return (v, None)

def back_low(kept, grad):
    return (low(grad),)
low.defvjp(low_keep, low_pass)
low_back.defvjp(back_keep, back_low)

def rms_rows(value):
    return value * lax.rsqrt(lax.optimization_barrier(jnp.mean(value * value, axis=-1, keepdims=True)) + epsilon)

def block_forward(inputs, in_weight, out_weight, gate_weight, up_weight, down_weight, mix_gain, ffn_gain, conv_taps):
    highest = lax.Precision.HIGHEST
    width = inputs.shape[-1]
    length = inputs.shape[0]
    normed = low(rms_rows(inputs) * mix_gain)
    mixed = low_back(jnp.dot(normed, in_weight, precision=highest))
    b_part = mixed[:, :width]
    c_part = mixed[:, width:2 * width]
    x_part = mixed[:, 2 * width:]
    product = low(b_part * x_part)
    padded = jnp.concatenate([jnp.zeros((2, width), jnp.float32), product], 0)
    conv = conv_taps[0] * padded[:length] + conv_taps[1] * padded[1:length + 1] + conv_taps[2] * padded[2:]
    gated = low(c_part * conv)
    branch = low_back(jnp.dot(gated, out_weight, precision=highest))
    resid = inputs + branch
    hnorm = low(rms_rows(resid) * ffn_gain)
    gate = low_back(jnp.dot(hnorm, gate_weight, precision=highest))
    upper = low_back(jnp.dot(hnorm, up_weight, precision=highest))
    hidden = low(jax.nn.silu(gate) * upper)
    return resid + low_back(jnp.dot(hidden, down_weight, precision=highest))

def reference(tokens, cotangent, in_weight, out_weight, gate_weight, up_weight, down_weight, mix_gain, ffn_gain, conv_taps):
    weights = tuple((w.astype(jnp.float32) for w in (in_weight, out_weight, gate_weight, up_weight, down_weight, mix_gain, ffn_gain, conv_taps)))

    def per_sequence(carry, pair):
        sequence, seq_cot = pair
        result, pull = jax.vjp(block_forward, sequence.astype(jnp.float32), *weights)
        grads = pull(seq_cot.astype(jnp.float32))
        summed = tuple((a + b for a, b in zip(carry, grads[1:])))
        return (summed, (result.astype(jnp.bfloat16), grads[0].astype(jnp.bfloat16)))
    initial = tuple((jnp.zeros(w.shape, jnp.float32) for w in weights))
    sums, pieces = lax.scan(per_sequence, initial, (tokens, cotangent))
    return (pieces[0], pieces[1], sums[0], sums[1], sums[2], sums[3], sums[4], sums[5], sums[6], sums[7])
```

```python
import jax
import jax.numpy as jnp
from jax import lax
from jax.sharding import Mesh, PartitionSpec as P

epsilon = 1e-05
PAIR = ((0, 1), (1, 0))


def ring_order(count):
    return list(range(0, count, 2)) + list(range(1, count, 2))[::-1]


def ring_pairs(count):
    order = ring_order(count)
    ahead = [(order[i], order[(i + 1) % count]) for i in range(count)]
    return ahead, [(b, a) for a, b in ahead]


def ring_place(count, offset):
    order = ring_order(count)
    position = [order.index(i) for i in range(count)]
    here = jnp.array(position, jnp.int32)[lax.axis_index("shard")]
    return jnp.array(order, jnp.int32)[(here + offset) % count]


def ring_gather(block, flip=False):
    count = lax.axis_size("shard")
    rows = block.shape[0]
    ahead, back = ring_pairs(count)
    sign = 1
    if flip:
        ahead, back, sign = back, ahead, -1
    far, near = count // 2, count - 1 - count // 2
    whole = jnp.zeros((count * rows, block.shape[1]), block.dtype)
    whole = lax.dynamic_update_slice(whole, block, (lax.axis_index("shard") * rows, 0))
    one = two = block
    for step in range(1, far + 1):
        one = lax.ppermute(one, "shard", ahead)
        whole = lax.dynamic_update_slice(whole, one, (ring_place(count, -sign * step) * rows, 0))
        if step <= near:
            two = lax.ppermute(two, "shard", back)
            whole = lax.dynamic_update_slice(whole, two, (ring_place(count, sign * step) * rows, 0))
    return whole


def ring_scatter(value, flip=False):
    count = lax.axis_size("shard")
    rows = value.shape[0] // count
    ahead, back = ring_pairs(count)
    sign = 1
    if flip:
        ahead, back, sign = back, ahead, -1
    far, near = count // 2, count - 1 - count // 2

    def part(offset):
        start = ring_place(count, offset) * rows
        return lax.dynamic_slice(value, (start, 0), (rows, value.shape[1])).astype(jnp.float32)

    one = part(sign * far).astype(jnp.bfloat16)
    two = part(-sign * near).astype(jnp.bfloat16)
    for step in range(far - 1, -1, -1):
        one = lax.ppermute(one, "shard", ahead)
        if step > 0:
            one = (one.astype(jnp.float32) + part(sign * step)).astype(jnp.bfloat16)
    for step in range(near - 1, -1, -1):
        two = lax.ppermute(two, "shard", back)
        if step > 0:
            two = (two.astype(jnp.float32) + part(-sign * step)).astype(jnp.bfloat16)
    return part(0) + one.astype(jnp.float32) + two.astype(jnp.float32)


def over_core(value):
    return lax.ppermute(value, "core", PAIR)


def over_y(value):
    return lax.ppermute(value, "y", PAIR)


def four_gather(value):
    beside = over_core(value)
    across = over_y(value)
    return jnp.concatenate([value, beside, across, over_core(across)], 0)


def four_scatter(value):
    rows = value.shape[0] // 4
    mine, beside, across, diagonal = (value[i * rows : (i + 1) * rows] for i in range(4))
    other = over_core(diagonal.astype(jnp.bfloat16)).astype(jnp.float32) + across
    received = over_y(other.astype(jnp.bfloat16)).astype(jnp.float32)
    near = over_core(beside.astype(jnp.bfloat16)).astype(jnp.float32)
    return mine + near + received


def outer_sum(left, right):
    return lax.dot_general(
        left, right, (((0,), (0,)), ((), ())), preferred_element_type=jnp.float32
    )


def times_transposed(grad, weight):
    return lax.dot_general(
        grad, weight, (((1,), (1,)), ((), ())), preferred_element_type=jnp.float32
    )


def times(value, weight):
    return jnp.dot(value, weight, preferred_element_type=jnp.float32)


def picked(value, groups, parts, part):
    size = value.shape[1] // (groups * parts)
    row = lax.broadcasted_iota(jnp.int32, (value.shape[1], groups * size), 0)
    column = lax.broadcasted_iota(jnp.int32, (value.shape[1], groups * size), 1)
    wanted = (column // size * parts + part) * size + column % size
    return times(value, (row == wanted).astype(value.dtype)).astype(value.dtype)


def local(
    tokens,
    cotangent,
    in_weight,
    out_weight,
    gate_weight,
    up_weight,
    down_weight,
    mix_gain,
    ffn_gain,
    conv_taps,
):
    shards = lax.axis_size("shard")
    core = lax.axis_index("core")
    member = lax.axis_index("y") * 2 + core
    width = tokens.shape[-1]
    length = tokens.shape[1]
    half = width // 2
    hidden_rows = down_weight.shape[0]

    small = jnp.concatenate([mix_gain[None], ffn_gain[None], conv_taps], 0)
    small_full = lax.all_gather(small, "shard", axis=1, tiled=True)
    in_mine = jnp.concatenate(
        [picked(in_weight[:, i * width : (i + 1) * width], shards, 2, core) for i in range(3)], 1
    )
    out_rows = out_weight.shape[0] // 2
    out_mine = lax.dynamic_slice(out_weight, (core * out_rows, 0), (out_rows, width))
    gate_mine = picked(gate_weight, shards, 4, member)
    up_mine = picked(up_weight, shards, 4, member)
    down_rows = hidden_rows // 4
    down_mine = lax.dynamic_slice(down_weight, (member * down_rows, 0), (down_rows, width))
    in_full = ring_gather(in_mine)
    out_full = ring_gather(out_mine, True)
    gate_full = ring_gather(gate_mine, True)
    up_full = ring_gather(up_mine)
    down_full = ring_gather(down_mine, True)

    params = small_full.astype(jnp.float32)
    gain_one = params[0]
    gain_two = params[1]
    taps = lax.dynamic_index_in_dim(
        params[2:5].reshape(3, shards, 2, half // shards), core, 2, keepdims=False
    ).reshape(3, half)

    inputs = tokens[0].astype(jnp.float32)
    factor_one = lax.rsqrt(jnp.mean(inputs * inputs, axis=-1, keepdims=True) + epsilon)
    unit_one = inputs * factor_one
    normed_own = (unit_one * gain_one).astype(jnp.bfloat16)
    normed = jnp.concatenate([normed_own, over_core(normed_own)], 0)
    mixed = times(normed, in_full)
    b_part = mixed[:, :half].reshape(2, length, half)
    c_part = mixed[:, half : 2 * half].reshape(2, length, half)
    x_part = mixed[:, 2 * half :].reshape(2, length, half)
    product = (b_part * x_part).astype(jnp.bfloat16)
    previous = lax.ppermute(
        product[:, length - 2 :], "shard", [(i, i + 1) for i in range(shards - 1)]
    )
    padded = jnp.concatenate([previous, product], 1).astype(jnp.float32)
    conv = (
        taps[0] * padded[:, :length] + taps[1] * padded[:, 1 : length + 1] + taps[2] * padded[:, 2:]
    )
    gated = (c_part * conv).astype(jnp.bfloat16).reshape(2 * length, half)
    branch = times(gated, out_full)
    resid = (
        inputs
        + branch[:length]
        + over_core(branch[length:].astype(jnp.bfloat16)).astype(jnp.float32)
    )

    factor_two = lax.rsqrt(jnp.mean(resid * resid, axis=-1, keepdims=True) + epsilon)
    unit_two = resid * factor_two
    hnorm = four_gather((unit_two * gain_two).astype(jnp.bfloat16))
    grad_rows = four_gather(cotangent[0])
    gate = times(hnorm, gate_full)
    upper = times(hnorm, up_full)
    sigma = jax.nn.sigmoid(gate)
    activated = gate * sigma
    hidden = (activated * upper).astype(jnp.bfloat16)
    d_hidden = times_transposed(grad_rows, down_full)
    d_gate = (d_hidden * upper * sigma * (1.0 + gate * (1.0 - sigma))).astype(jnp.bfloat16)
    d_up = (d_hidden * activated).astype(jnp.bfloat16)
    d_hnorm = four_scatter(times_transposed(d_gate, gate_full) + times_transposed(d_up, up_full))
    g_down = ring_scatter(outer_sum(hidden, grad_rows))
    g_gate = ring_scatter(outer_sum(hnorm, d_gate), True)
    g_up = ring_scatter(outer_sum(hnorm, d_up))
    output = (resid + four_scatter(times(hidden, down_full))).astype(jnp.bfloat16)

    g_ffn_gain = jnp.sum(d_hnorm * unit_two, axis=0)
    scaled_two = d_hnorm * gain_two
    d_resid = cotangent[0].astype(jnp.float32) + factor_two * (
        scaled_two - unit_two * jnp.mean(scaled_two * unit_two, axis=-1, keepdims=True)
    )

    d_own = d_resid.astype(jnp.bfloat16)
    d_branch = jnp.concatenate([d_own, over_core(d_own)], 0)
    d_gated = times_transposed(d_branch, out_full).reshape(2, length, half)
    g_out = ring_scatter(outer_sum(gated, d_branch), True)
    d_cpart = d_gated * conv
    d_conv = d_gated * c_part
    tap_grads = jnp.stack(
        [jnp.sum(d_conv * padded[:, k : k + length], axis=(0, 1)) for k in range(3)], 0
    )
    spread = (
        jnp.pad(taps[0] * d_conv, ((0, 0), (0, 2), (0, 0)))
        + jnp.pad(taps[1] * d_conv, ((0, 0), (1, 1), (0, 0)))
        + jnp.pad(taps[2] * d_conv, ((0, 0), (2, 0), (0, 0)))
    )
    returned = lax.ppermute(spread[:, :2], "shard", [(i + 1, i) for i in range(shards - 1)])
    d_product = spread[:, 2:].at[:, length - 2 :].add(returned)
    d_mixed = (
        jnp.concatenate([d_product * x_part, d_cpart, d_product * b_part], -1)
        .astype(jnp.bfloat16)
        .reshape(2 * length, 3 * half)
    )
    d_normed = times_transposed(d_mixed, in_full)
    g_in = ring_scatter(outer_sum(normed, d_mixed))
    d_normed = d_normed[:length] + over_core(d_normed[length:].astype(jnp.bfloat16)).astype(
        jnp.float32
    )
    g_mix_gain = jnp.sum(d_normed * unit_one, axis=0)
    scaled_one = d_normed * gain_one
    d_inputs = d_resid + factor_one * (
        scaled_one - unit_one * jnp.mean(scaled_one * unit_one, axis=-1, keepdims=True)
    )

    def summed(value):
        return lax.psum(value, "outer") if lax.axis_size("outer") > 1 else value

    def four_parts(value):
        rows = value.shape[0]
        found = four_gather(summed(value).astype(jnp.bfloat16)).reshape(4, rows, value.shape[1])
        y_bit, c_bit = member // 2, core
        found = jnp.where(c_bit == 1, found[jnp.array([1, 0, 3, 2])], found)
        return jnp.where(y_bit == 1, found[jnp.array([2, 3, 0, 1])], found)

    def spread_four(value):
        rows = value.shape[0]
        parts = four_parts(value).reshape(4, rows, shards, down_rows)
        return parts.transpose(1, 2, 0, 3).reshape(rows, -1).astype(jnp.float32)

    def two_parts(value):
        mine = summed(value).astype(jnp.bfloat16)
        mine = (mine.astype(jnp.float32) + over_y(mine).astype(jnp.float32)).astype(jnp.bfloat16)
        other = over_core(mine)
        return jnp.where(core == 0, jnp.stack([mine, other]), jnp.stack([other, mine]))

    owned_in = two_parts(g_in).reshape(2, -1, 3, shards, half // shards)
    owned_in = owned_in.transpose(1, 2, 3, 0, 4).reshape(-1, 3 * width).astype(jnp.float32)
    owned_out = two_parts(g_out).reshape(-1, width).astype(jnp.float32)
    owned_down = four_parts(g_down).reshape(-1, width).astype(jnp.float32)
    spot = lax.broadcasted_iota(jnp.int32, (3, shards, 2, half // shards), 2)
    tap_full = jnp.where(
        spot == core, tap_grads.reshape(3, shards, 1, half // shards), 0.0
    ).reshape(3, width)
    small_grads = jnp.concatenate([g_mix_gain[None], g_ffn_gain[None], tap_full], 0)
    small_grads = lax.psum(small_grads, ("shard", "outer", "y", "core"))
    own = width // shards
    small_owned = lax.dynamic_slice(small_grads, (0, lax.axis_index("shard") * own), (5, own))
    return (
        output[None],
        d_inputs.astype(jnp.bfloat16)[None],
        owned_in,
        owned_out,
        spread_four(g_gate),
        spread_four(g_up),
        owned_down,
        small_owned[0],
        small_owned[1],
        small_owned[2:5],
    )


def solution(mesh):
    shards = mesh.shape["shard"]
    reps = mesh.shape["rep"]
    finer = Mesh(mesh.devices.reshape(shards, reps // 4, 2, 2), ("shard", "outer", "y", "core"))
    rep = ("outer", "y", "core")
    in_specs = (
        P(rep, "shard", None),
        P(rep, "shard", None),
        P("shard", None),
        P("shard", None),
        P("shard", None),
        P("shard", None),
        P("shard", None),
        P("shard"),
        P("shard"),
        P(None, "shard"),
    )
    return jax.shard_map(
        local, mesh=finer, in_specs=in_specs, out_specs=in_specs, check_vma=False
    )
```

```python
import functools

import jax
import jax.numpy as jnp
from jax import lax
from jax.experimental import pallas as pl
from jax.experimental.pallas import tpu as pltpu
from jax.sharding import Mesh, PartitionSpec as P

epsilon = 1e-05
PAIR = ((0, 1), (1, 0))


def ring_order(count):
    return list(range(0, count, 2)) + list(range(1, count, 2))[::-1]


def ring_pairs(count):
    order = ring_order(count)
    ahead = [(order[i], order[(i + 1) % count]) for i in range(count)]
    return ahead, [(b, a) for a, b in ahead]


def ring_place(count, offset):
    order = ring_order(count)
    position = [order.index(i) for i in range(count)]
    here = jnp.array(position, jnp.int32)[lax.axis_index("shard")]
    return jnp.array(order, jnp.int32)[(here + offset) % count]


def ring_gather(block, flip=False):
    count = lax.axis_size("shard")
    rows = block.shape[0]
    ahead, back = ring_pairs(count)
    sign = 1
    if flip:
        ahead, back, sign = back, ahead, -1
    far, near = count // 2, count - 1 - count // 2
    whole = jnp.zeros((count * rows, block.shape[1]), block.dtype)
    whole = lax.dynamic_update_slice(whole, block, (lax.axis_index("shard") * rows, 0))
    one = two = block
    for step in range(1, far + 1):
        one = lax.ppermute(one, "shard", ahead)
        whole = lax.dynamic_update_slice(whole, one, (ring_place(count, -sign * step) * rows, 0))
        if step <= near:
            two = lax.ppermute(two, "shard", back)
            whole = lax.dynamic_update_slice(whole, two, (ring_place(count, sign * step) * rows, 0))
    return whole


def ring_scatter(value, flip=False):
    count = lax.axis_size("shard")
    rows = value.shape[0] // count
    ahead, back = ring_pairs(count)
    sign = 1
    if flip:
        ahead, back, sign = back, ahead, -1
    far, near = count // 2, count - 1 - count // 2

    def part(offset):
        start = ring_place(count, offset) * rows
        return lax.dynamic_slice(value, (start, 0), (rows, value.shape[1])).astype(jnp.float32)

    one = part(sign * far).astype(jnp.bfloat16)
    two = part(-sign * near).astype(jnp.bfloat16)
    for step in range(far - 1, -1, -1):
        one = lax.ppermute(one, "shard", ahead)
        if step > 0:
            one = (one.astype(jnp.float32) + part(sign * step)).astype(jnp.bfloat16)
    for step in range(near - 1, -1, -1):
        two = lax.ppermute(two, "shard", back)
        if step > 0:
            two = (two.astype(jnp.float32) + part(-sign * step)).astype(jnp.bfloat16)
    return part(0) + one.astype(jnp.float32) + two.astype(jnp.float32)


def over_core(value):
    return lax.ppermute(value, "core", PAIR)


def over_y(value):
    return lax.ppermute(value, "y", PAIR)


def four_gather(value):
    beside = over_core(value)
    across = over_y(value)
    return jnp.concatenate([value, beside, across, over_core(across)], 0)


def four_scatter(value):
    rows = value.shape[0] // 4
    mine, beside, across, diagonal = (value[i * rows : (i + 1) * rows] for i in range(4))
    other = over_core(diagonal.astype(jnp.bfloat16)).astype(jnp.float32) + across
    received = over_y(other.astype(jnp.bfloat16)).astype(jnp.float32)
    near = over_core(beside.astype(jnp.bfloat16)).astype(jnp.float32)
    return mine + near + received


def lay_out_kernel(groups, member_ref, parts_ref, out_ref):
    member = member_ref[0]
    size = parts_ref.shape[2] // groups
    for place in range(4):
        part = parts_ref[jnp.bitwise_xor(place, member)].astype(jnp.float32)
        for group in range(groups):
            start = (group * 4 + place) * size
            out_ref[:, start : start + size] = part[:, group * size : (group + 1) * size]


def lay_out(parts, member, groups):
    rows, columns = parts.shape[1:]
    return pl.pallas_call(
        functools.partial(lay_out_kernel, groups),
        out_shape=jax.ShapeDtypeStruct((rows, 4 * columns), jnp.float32),
        in_specs=[
            pl.BlockSpec(memory_space=pltpu.SMEM),
            pl.BlockSpec(memory_space=pltpu.VMEM),
        ],
        out_specs=pl.BlockSpec(memory_space=pltpu.VMEM),
        compiler_params=pltpu.CompilerParams(vmem_limit_bytes=32 * 2**20),
        cost_estimate=pl.CostEstimate(flops=0, bytes_accessed=24 * rows * columns, transcendentals=0),
    )(member[None], parts)


def outer_sum(left, right):
    return lax.dot_general(
        left, right, (((0,), (0,)), ((), ())), preferred_element_type=jnp.float32
    )


def times_transposed(grad, weight):
    return lax.dot_general(
        grad, weight, (((1,), (1,)), ((), ())), preferred_element_type=jnp.float32
    )


def times(value, weight):
    return jnp.dot(value, weight, preferred_element_type=jnp.float32)


def picked(value, groups, parts, part):
    size = value.shape[1] // (groups * parts)
    row = lax.broadcasted_iota(jnp.int32, (value.shape[1], groups * size), 0)
    column = lax.broadcasted_iota(jnp.int32, (value.shape[1], groups * size), 1)
    wanted = (column // size * parts + part) * size + column % size
    return times(value, (row == wanted).astype(value.dtype)).astype(value.dtype)


def local(
    tokens,
    cotangent,
    in_weight,
    out_weight,
    gate_weight,
    up_weight,
    down_weight,
    mix_gain,
    ffn_gain,
    conv_taps,
):
    shards = lax.axis_size("shard")
    core = lax.axis_index("core")
    member = lax.axis_index("y") * 2 + core
    width = tokens.shape[-1]
    length = tokens.shape[1]
    half = width // 2
    hidden_rows = down_weight.shape[0]

    small = jnp.concatenate([mix_gain[None], ffn_gain[None], conv_taps], 0)
    own = small.shape[1]
    in_mine = jnp.concatenate(
        [picked(in_weight[:, i * width : (i + 1) * width], shards, 2, core) for i in range(3)], 1
    )
    out_rows = out_weight.shape[0] // 2
    out_mine = lax.dynamic_slice(out_weight, (core * out_rows, 0), (out_rows, width))
    out_mine = jnp.concatenate([out_mine[:, :half], out_mine[:, half:]], 0)
    small_rows = jnp.pad(small, ((0, 11), (0, 4 * half - own)))
    mix_mine = jnp.concatenate([jnp.concatenate([in_mine, out_mine], 1), small_rows], 0)
    mix_full = ring_gather(mix_mine).reshape(shards, own + 16, 4 * half)
    in_full = mix_full[:, :own, : 3 * half].reshape(width, 3 * half)
    out_full = mix_full[:, :own, 3 * half :].reshape(shards, 2, out_rows, half)
    out_full = out_full.transpose(0, 2, 1, 3).reshape(half, width)
    small_full = mix_full[:, own : own + 5, :own].transpose(1, 0, 2).reshape(5, width)

    quarter = hidden_rows * shards // 4
    both_mine = jnp.concatenate(
        [picked(gate_weight, shards, 4, member), picked(up_weight, shards, 4, member)], 1
    )
    down_rows = hidden_rows // 4
    down_mine = lax.dynamic_slice(down_weight, (member * down_rows, 0), (down_rows, width))
    both_full = ring_gather(both_mine, True)
    down_full = ring_gather(down_mine)

    params = small_full.astype(jnp.float32)
    gain_one = params[0]
    gain_two = params[1]
    taps = lax.dynamic_index_in_dim(
        params[2:5].reshape(3, shards, 2, half // shards), core, 2, keepdims=False
    ).reshape(3, half)

    pair = jnp.concatenate([tokens[0], over_core(tokens[0])], 0).astype(jnp.float32)
    factor_pair = lax.rsqrt(jnp.mean(pair * pair, axis=-1, keepdims=True) + epsilon)
    unit_pair = pair * factor_pair
    normed = (unit_pair * gain_one).astype(jnp.bfloat16)
    inputs, factor_one, unit_one = pair[:length], factor_pair[:length], unit_pair[:length]
    mixed = times(normed, in_full)
    b_part = mixed[:, :half].reshape(2, length, half)
    c_part = mixed[:, half : 2 * half].reshape(2, length, half)
    x_part = mixed[:, 2 * half :].reshape(2, length, half)
    product = (b_part * x_part).astype(jnp.bfloat16)
    previous = lax.ppermute(
        product[:, length - 2 :], "shard", [(i, i + 1) for i in range(shards - 1)]
    )
    padded = jnp.concatenate([previous, product], 1).astype(jnp.float32)
    conv = (
        taps[0] * padded[:, :length] + taps[1] * padded[:, 1 : length + 1] + taps[2] * padded[:, 2:]
    )
    gated = (c_part * conv).astype(jnp.bfloat16).reshape(2 * length, half)
    branch = times(gated, out_full)
    resid = (
        inputs
        + branch[:length]
        + over_core(branch[length:].astype(jnp.bfloat16)).astype(jnp.float32)
    )

    factor_two = lax.rsqrt(jnp.mean(resid * resid, axis=-1, keepdims=True) + epsilon)
    unit_two = resid * factor_two
    hnorm = four_gather((unit_two * gain_two).astype(jnp.bfloat16))
    grad_rows = four_gather(cotangent[0])
    mid = times(hnorm, both_full)
    gate = mid[:, :quarter]
    upper = mid[:, quarter:]
    sigma = jax.nn.sigmoid(gate)
    activated = gate * sigma
    hidden = (activated * upper).astype(jnp.bfloat16)
    d_hidden = times_transposed(grad_rows, down_full)
    d_gate = (d_hidden * upper * sigma * (1.0 + gate * (1.0 - sigma))).astype(jnp.bfloat16)
    d_up = (d_hidden * activated).astype(jnp.bfloat16)
    d_both = jnp.concatenate([d_gate, d_up], 1)
    d_hnorm = four_scatter(times_transposed(d_both, both_full))
    g_down = ring_scatter(outer_sum(hidden, grad_rows))
    g_both = ring_scatter(outer_sum(hnorm, d_both), True)
    output = (resid + four_scatter(times(hidden, down_full))).astype(jnp.bfloat16)

    g_ffn_gain = jnp.sum(d_hnorm * unit_two, axis=0)
    scaled_two = d_hnorm * gain_two
    d_resid = cotangent[0].astype(jnp.float32) + factor_two * (
        scaled_two - unit_two * jnp.mean(scaled_two * unit_two, axis=-1, keepdims=True)
    )

    d_own = d_resid.astype(jnp.bfloat16)
    d_branch = jnp.concatenate([d_own, over_core(d_own)], 0)
    d_gated = times_transposed(d_branch, out_full).reshape(2, length, half)
    g_out = outer_sum(gated, d_branch)
    d_cpart = d_gated * conv
    d_conv = d_gated * c_part
    tap_grads = jnp.stack(
        [jnp.sum(d_conv * padded[:, k : k + length], axis=(0, 1)) for k in range(3)], 0
    )
    spread = (
        jnp.pad(taps[0] * d_conv, ((0, 0), (0, 2), (0, 0)))
        + jnp.pad(taps[1] * d_conv, ((0, 0), (1, 1), (0, 0)))
        + jnp.pad(taps[2] * d_conv, ((0, 0), (2, 0), (0, 0)))
    )
    returned = lax.ppermute(spread[:, :2], "shard", [(i + 1, i) for i in range(shards - 1)])
    d_product = spread[:, 2:].at[:, length - 2 :].add(returned)
    d_mixed = (
        jnp.concatenate([d_product * x_part, d_cpart, d_product * b_part], -1)
        .astype(jnp.bfloat16)
        .reshape(2 * length, 3 * half)
    )
    d_normed = times_transposed(d_mixed, in_full)
    g_in = outer_sum(normed, d_mixed)
    g_mix_gain = jnp.sum(d_normed * unit_pair, axis=0)
    spot = lax.broadcasted_iota(jnp.int32, (3, shards, 2, half // shards), 2)
    tap_full = jnp.where(
        spot == core, tap_grads.reshape(3, shards, 1, half // shards), 0.0
    ).reshape(3, width)
    small_grads = jnp.concatenate([g_mix_gain[None], g_ffn_gain[None], tap_full], 0)
    small_grads = jnp.pad(
        small_grads.reshape(5, shards, own).transpose(1, 0, 2),
        ((0, 0), (0, 11), (0, 4 * half - own)),
    )
    g_out = g_out.reshape(shards, out_rows, 2, half).transpose(0, 2, 1, 3)
    g_mix = jnp.concatenate(
        [g_in.reshape(shards, own, 3 * half), g_out.reshape(shards, own, half)], 2
    )
    g_mix = jnp.concatenate([g_mix, small_grads], 1).reshape(shards * (own + 16), 4 * half)
    g_mix = ring_scatter(g_mix)
    d_normed = d_normed[:length] + over_core(d_normed[length:].astype(jnp.bfloat16)).astype(
        jnp.float32
    )
    scaled_one = d_normed * gain_one
    d_inputs = d_resid + factor_one * (
        scaled_one - unit_one * jnp.mean(scaled_one * unit_one, axis=-1, keepdims=True)
    )

    def summed(value):
        return lax.psum(value, "outer") if lax.axis_size("outer") > 1 else value

    def four_parts(value):
        found = four_gather(summed(value).astype(jnp.bfloat16))
        return found.reshape(4, value.shape[0], value.shape[1])

    both_parts = four_parts(g_both)
    owned_gate = lay_out(both_parts[:, :, :quarter], member, shards)
    owned_up = lay_out(both_parts[:, :, quarter:], member, shards)
    down_parts = four_parts(g_down)
    owned_down = jnp.concatenate(
        [
            lax.dynamic_index_in_dim(down_parts, jnp.bitwise_xor(i, member), 0, keepdims=False)
            for i in range(4)
        ],
        0,
    ).astype(jnp.float32)

    mix_mine = summed(g_mix).astype(jnp.bfloat16)
    mix_mine = mix_mine.astype(jnp.float32) + over_y(mix_mine).astype(jnp.float32)
    mix_mine = mix_mine.astype(jnp.bfloat16)
    mix_other = over_core(mix_mine)
    low = jnp.where(core == 0, mix_mine, mix_other)
    high = jnp.where(core == 0, mix_other, mix_mine)
    size = half // shards
    owned_in = jnp.stack(
        [value[:own, : 3 * half].reshape(own, 3 * shards, size) for value in (low, high)], 2
    )
    owned_in = owned_in.reshape(own, 3 * width).astype(jnp.float32)
    owned_out = jnp.concatenate(
        [
            jnp.concatenate([value[:out_rows, 3 * half :], value[out_rows:own, 3 * half :]], 1)
            for value in (low, high)
        ],
        0,
    ).astype(jnp.float32)
    small_owned = low[own : own + 5, :own].astype(jnp.float32) + high[own : own + 5, :own].astype(
        jnp.float32
    )
    return (
        output[None],
        d_inputs.astype(jnp.bfloat16)[None],
        owned_in,
        owned_out,
        owned_gate,
        owned_up,
        owned_down,
        small_owned[0],
        small_owned[1],
        small_owned[2:5],
    )


def solution(mesh):
    shards = mesh.shape["shard"]
    reps = mesh.shape["rep"]
    finer = Mesh(mesh.devices.reshape(shards, reps // 4, 2, 2), ("shard", "outer", "y", "core"))
    rep = ("outer", "y", "core")
    in_specs = (
        P(rep, "shard", None),
        P(rep, "shard", None),
        P("shard", None),
        P("shard", None),
        P("shard", None),
        P("shard", None),
        P("shard", None),
        P("shard"),
        P("shard"),
        P(None, "shard"),
    )
    return jax.shard_map(
        local, mesh=finer, in_specs=in_specs, out_specs=in_specs, check_vma=False
    )
```

```python
import functools

import jax
import jax.numpy as jnp
from jax import lax
from jax.experimental import pallas as pl
from jax.experimental.pallas import tpu as pltpu
from jax.sharding import Mesh, PartitionSpec as P

epsilon = 1e-05
PAIR = ((0, 1), (1, 0))


def over_core(value):
    return lax.ppermute(value, "core", PAIR)


def over_y(value):
    return lax.ppermute(value, "y", PAIR)


def outer_sum(left, right):
    return lax.dot_general(
        left, right, (((0,), (0,)), ((), ())), preferred_element_type=jnp.float32
    )


def times_transposed(grad, weight):
    return lax.dot_general(
        grad, weight, (((1,), (1,)), ((), ())), preferred_element_type=jnp.float32
    )


def times(value, weight):
    return jnp.dot(value, weight, preferred_element_type=jnp.float32)


def wide(value):
    return value.astype(jnp.float32)


def narrow(value):
    return value.astype(jnp.bfloat16)


def tie_kernel(*refs):
    del refs


def tie(value, *others):
    return pl.pallas_call(
        tie_kernel,
        out_shape=jax.ShapeDtypeStruct(value.shape, value.dtype),
        in_specs=[pl.BlockSpec(memory_space=pl.ANY)] * (1 + len(others)),
        out_specs=pl.BlockSpec(memory_space=pl.ANY),
        input_output_aliases={0: 0},
    )(value, *others)


def ring_order(count):
    return list(range(0, count, 2)) + list(range(1, count, 2))[::-1]


def ring_pairs(count):
    order = ring_order(count)
    ahead = [(order[i], order[(i + 1) % count]) for i in range(count)]
    return ahead, [(b, a) for a, b in ahead]


def ring_place(count, offset):
    me = lax.axis_index("shard")
    here = jnp.where(me % 2 == 0, me // 2, count - 1 - me // 2)
    there = (here + offset) % count
    return jnp.where(there < count // 2, 2 * there, 2 * (count - 1 - there) + 1)


class Gather:
    def __init__(self, block, flip):
        self.count = lax.axis_size("shard")
        self.far, self.near = self.count // 2, self.count - 1 - self.count // 2
        self.sign = -1 if flip else 1
        self.pairs = ring_pairs(self.count)[:: self.sign]
        self.step = 0
        self.one = self.two = block
        self.whole = jnp.zeros((self.count,) + block.shape, block.dtype)
        self.put(block, 0)

    def put(self, block, offset):
        place = ring_place(self.count, offset)
        self.whole = lax.dynamic_update_slice(self.whole, block[None], (place, 0, 0))

    def hop(self):
        self.step += 1
        if self.step <= self.far:
            self.one = lax.ppermute(self.one, "shard", self.pairs[0])
            self.put(self.one, -self.sign * self.step)
        if self.step <= self.near:
            self.two = lax.ppermute(self.two, "shard", self.pairs[1])
            self.put(self.two, self.sign * self.step)
        return self

    def end(self):
        while self.step < self.far:
            self.hop()
        return self.whole


class Scatter:
    def __init__(self, part, flip):
        self.count = lax.axis_size("shard")
        self.far, self.near = self.count // 2, self.count - 1 - self.count // 2
        self.sign = -1 if flip else 1
        self.pairs = ring_pairs(self.count)[:: self.sign]
        self.step = 0
        self.part = lambda offset: wide(part(ring_place(self.count, offset)))
        self.one = narrow(self.part(self.sign * self.far))
        self.two = narrow(self.part(-self.sign * self.near))

    def hop(self):
        self.step += 1
        if self.step <= self.far:
            self.one = lax.ppermute(self.one, "shard", self.pairs[0])
            if self.step < self.far:
                self.one = narrow(wide(self.one) + self.part(self.sign * (self.far - self.step)))
        if self.step <= self.near:
            self.two = lax.ppermute(self.two, "shard", self.pairs[1])
            if self.step < self.near:
                self.two = narrow(wide(self.two) + self.part(-self.sign * (self.near - self.step)))
        return self

    def end(self):
        while self.step < self.far:
            self.hop()
        return self.part(0) + wide(self.one) + wide(self.two)


def rows_block(tile, columns, first=0):
    return pl.BlockSpec((tile, columns), lambda i: (first + i, 0))


def whole_block(shape):
    zeros = (0,) * len(shape)
    return pl.BlockSpec(shape, lambda i: zeros, pipeline_mode=pl.Buffered(1))


def params(size=48):
    return pltpu.CompilerParams(vmem_limit_bytes=size * 2**20)


def flat(value):
    return value.reshape(-1, value.shape[-1])


def mix_in_kernel(half, own, tokens_ref, gain_ref, mix_ref, normed_ref, b_ref, c_ref, x_ref, p_ref):
    inputs = wide(tokens_ref[...])
    unit = inputs * lax.rsqrt(jnp.mean(inputs * inputs, axis=-1, keepdims=True) + epsilon)
    normed = narrow(unit * gain_ref[...])
    normed_ref[...] = normed
    for i, ref in enumerate((b_ref, c_ref, x_ref)):
        ref[...] = times(normed, flat(mix_ref[:, :own, i * half : (i + 1) * half]))
    p_ref[...] = narrow(b_ref[...] * x_ref[...])


def mix_in(tokens, gain, mix, own):
    count, width = tokens.shape
    half = width // 2
    tile = count // 4
    f32, bf16 = jnp.float32, jnp.bfloat16
    shapes = [(width, bf16), (half, f32), (half, f32), (half, f32), (half, bf16)]
    return pl.pallas_call(
        functools.partial(mix_in_kernel, half, own),
        grid=(4,),
        in_specs=[rows_block(tile, width), whole_block((1, width)), whole_block(mix.shape)],
        out_specs=[rows_block(tile, columns) for columns, _ in shapes],
        out_shape=[jax.ShapeDtypeStruct((count, columns), kind) for columns, kind in shapes],
        compiler_params=params(),
        cost_estimate=pl.CostEstimate(
            flops=6 * count * width * half, bytes_accessed=14 * count * width, transcendentals=0
        ),
    )(tokens, gain, mix)


def delayed(product, halo):
    row = lax.broadcasted_iota(jnp.int32, product.shape, 0)
    one = jnp.where(row == 0, halo[1:2], pltpu.roll(product, 1, 0))
    two = jnp.where(row == 0, halo[0:1], jnp.where(row == 1, halo[1:2], pltpu.roll(product, 2, 0)))
    return one, two


def mix_out_kernel(half, own, c_ref, p_ref, halo_ref, taps_ref, mix_ref, conv_ref, gated_ref, out_ref):
    product = wide(p_ref[...])
    one, two = delayed(product, wide(halo_ref[0]))
    conv = taps_ref[0:1] * two + taps_ref[1:2] * one + taps_ref[2:3] * product
    conv_ref[...] = conv
    gated = narrow(c_ref[...] * conv)
    gated_ref[...] = gated
    for i in range(2):
        weight = flat(mix_ref[:, i * own // 2 : (i + 1) * own // 2, 3 * half :])
        out_ref[:, i * half : (i + 1) * half] = narrow(times(gated, weight))


def mix_out(c_part, product, halo, taps, mix, own):
    count, half = product.shape
    length = count // 2
    shapes = [(half, jnp.float32), (half, jnp.bfloat16), (2 * half, jnp.bfloat16)]
    return pl.pallas_call(
        functools.partial(mix_out_kernel, half, own),
        grid=(2,),
        in_specs=[
            rows_block(length, half),
            rows_block(length, half),
            pl.BlockSpec((1,) + halo.shape[1:], lambda i: (i, 0, 0)),
            whole_block(taps.shape),
            whole_block(mix.shape),
        ],
        out_specs=[rows_block(length, columns) for columns, _ in shapes],
        out_shape=[jax.ShapeDtypeStruct((count, columns), kind) for columns, kind in shapes],
        compiler_params=params(),
        cost_estimate=pl.CostEstimate(
            flops=4 * count * half * half, bytes_accessed=16 * count * half, transcendentals=0
        ),
    )(c_part, product, halo, taps, mix)


def mix_back_kernel(
    half, own, d_ref, c_ref, conv_ref, p_ref, halo_ref, taps_ref, mix_ref, d_c_ref, d_p_ref, edge_ref, sums_ref
):
    grad = d_ref[...]
    d_gated = times_transposed(grad[:, :half], flat(mix_ref[:, : own // 2, 3 * half :]))
    d_gated += times_transposed(grad[:, half:], flat(mix_ref[:, own // 2 : own, 3 * half :]))
    d_c_ref[...] = narrow(d_gated * conv_ref[...])
    d_conv = d_gated * c_ref[...]
    product = wide(p_ref[...])
    one, two = delayed(product, wide(halo_ref[0]))

    @pl.when(pl.program_id(0) == 0)
    def _():
        sums_ref[...] = jnp.zeros_like(sums_ref)

    for k, value in enumerate((two, one, product)):
        sums_ref[k : k + 1] += jnp.sum(d_conv * value, axis=0, keepdims=True)
    taps = taps_ref[...]
    length = d_conv.shape[0]
    row = lax.broadcasted_iota(jnp.int32, d_conv.shape, 0)
    later = jnp.where(row < length - 1, pltpu.roll(d_conv, length - 1, 0), 0.0)
    latest = jnp.where(row < length - 2, pltpu.roll(d_conv, length - 2, 0), 0.0)
    d_p_ref[...] = taps[2:3] * d_conv + taps[1:2] * later + taps[0:1] * latest
    edge_ref[0, 0:1] = taps[0:1] * d_conv[0:1]
    edge_ref[0, 1:2] = taps[0:1] * d_conv[1:2] + taps[1:2] * d_conv[0:1]


def mix_back(d_branch, c_part, conv, product, halo, taps, mix, own):
    count, half = product.shape
    length = count // 2
    f32 = jnp.float32
    return pl.pallas_call(
        functools.partial(mix_back_kernel, half, own),
        grid=(2,),
        in_specs=[
            rows_block(length, 2 * half),
            rows_block(length, half),
            rows_block(length, half),
            rows_block(length, half),
            pl.BlockSpec((1,) + halo.shape[1:], lambda i: (i, 0, 0)),
            whole_block(taps.shape),
            whole_block(mix.shape),
        ],
        out_specs=[
            rows_block(length, half),
            rows_block(length, half),
            pl.BlockSpec((1, 2, half), lambda i: (i, 0, 0)),
            pl.BlockSpec((3, half), lambda i: (0, 0)),
        ],
        out_shape=[
            jax.ShapeDtypeStruct((count, half), jnp.bfloat16),
            jax.ShapeDtypeStruct((count, half), f32),
            jax.ShapeDtypeStruct((2, 2, half), f32),
            jax.ShapeDtypeStruct((3, half), f32),
        ],
        compiler_params=params(),
        cost_estimate=pl.CostEstimate(
            flops=4 * count * half * half, bytes_accessed=20 * count * half, transcendentals=0
        ),
    )(d_branch, c_part, conv, product, halo, taps, mix)


def mix_last_kernel(
    half, own, d_p_ref, edge_ref, b_ref, x_ref, d_c_ref, tokens_ref, mix_ref, d_mixed_ref, d_n_ref, sums_ref
):
    d_product = d_p_ref[...]
    length = d_product.shape[0]
    row = lax.broadcasted_iota(jnp.int32, d_product.shape, 0)
    edge = edge_ref[0]
    d_product += jnp.where(
        row == length - 2, edge[0:1], jnp.where(row == length - 1, edge[1:2], 0.0)
    )
    d_mixed_ref[:, :half] = narrow(d_product * x_ref[...])
    d_mixed_ref[:, half : 2 * half] = d_c_ref[...]
    d_mixed_ref[:, 2 * half :] = narrow(d_product * b_ref[...])
    d_normed = times_transposed(d_mixed_ref[...], flat(mix_ref[:, :own, : 3 * half]))
    d_n_ref[...] = narrow(d_normed)
    inputs = wide(tokens_ref[...])
    unit = inputs * lax.rsqrt(jnp.mean(inputs * inputs, axis=-1, keepdims=True) + epsilon)

    @pl.when(pl.program_id(0) == 0)
    def _():
        sums_ref[...] = jnp.zeros_like(sums_ref)

    sums_ref[...] += jnp.sum(d_normed * unit, axis=0, keepdims=True)


def mix_last(d_product, edge, b_part, x_part, d_c, tokens, mix, own):
    count, half = d_product.shape
    length = count // 2
    return pl.pallas_call(
        functools.partial(mix_last_kernel, half, own),
        grid=(2,),
        in_specs=[
            rows_block(length, half),
            pl.BlockSpec((1, 2, half), lambda i: (i, 0, 0)),
            rows_block(length, half),
            rows_block(length, half),
            rows_block(length, half),
            rows_block(length, 2 * half),
            whole_block(mix.shape),
        ],
        out_specs=[
            rows_block(length, 3 * half),
            rows_block(length, 2 * half),
            pl.BlockSpec((1, 2 * half), lambda i: (0, 0)),
        ],
        out_shape=[
            jax.ShapeDtypeStruct((count, 3 * half), jnp.bfloat16),
            jax.ShapeDtypeStruct((count, 2 * half), jnp.bfloat16),
            jax.ShapeDtypeStruct((1, 2 * half), jnp.float32),
        ],
        compiler_params=params(),
        cost_estimate=pl.CostEstimate(
            flops=12 * count * half * half, bytes_accessed=28 * count * half, transcendentals=0
        ),
    )(d_product, edge, b_part, x_part, d_c, tokens, mix)


def feed_forward_kernel(size, rows_ref, cot_ref, both_ref, down_ref, *refs):
    hidden_ref, d_both_ref, d_rows_ref, out_ref = refs[-4:]
    rows = rows_ref[...]
    cot = cot_ref[...]
    for start in range(0, size, 256):
        stop = min(start + 256, size)
        gate = times(rows, both_ref[:, start:stop])
        upper = times(rows, both_ref[:, size + start : size + stop])
        d_hidden = times_transposed(cot, down_ref[start:stop])
        sigma = jax.nn.sigmoid(gate)
        activated = gate * sigma
        hidden_ref[:, start:stop] = narrow(activated * upper)
        d_both_ref[:, start:stop] = narrow(d_hidden * upper * sigma * (1.0 + gate * (1.0 - sigma)))
        d_both_ref[:, size + start : size + stop] = narrow(d_hidden * activated)
    d_rows_ref[...] = narrow(times_transposed(d_both_ref[...], both_ref[...]))
    out_ref[...] = narrow(times(hidden_ref[...], down_ref[...]))


def feed_forward(rows, cot, both, down, at, kept=(), first=()):
    width = rows.shape[1]
    tokens = cot.shape[0] // 2
    tile = tokens // 2
    size = down.shape[0]
    here = 2 * at
    aliases = {4 + i: i for i in range(len(kept))}
    return pl.pallas_call(
        functools.partial(feed_forward_kernel, size),
        grid=(2,),
        in_specs=[
            rows_block(tile, width, here),
            rows_block(tile, width, here),
            whole_block(both.shape),
            whole_block(down.shape),
        ]
        + [pl.BlockSpec(memory_space=pl.ANY)] * (len(kept) + len(first)),
        out_specs=[
            rows_block(tile, size, here),
            rows_block(tile, 2 * size, here),
            rows_block(tile, width),
            rows_block(tile, width),
        ],
        out_shape=[
            jax.ShapeDtypeStruct((2 * tokens, size), jnp.bfloat16),
            jax.ShapeDtypeStruct((2 * tokens, 2 * size), jnp.bfloat16),
            jax.ShapeDtypeStruct((tokens, width), jnp.bfloat16),
            jax.ShapeDtypeStruct((tokens, width), jnp.bfloat16),
        ],
        input_output_aliases=aliases,
        compiler_params=params(),
        cost_estimate=pl.CostEstimate(
            flops=12 * tokens * width * size,
            bytes_accessed=16 * tokens * width,
            transcendentals=tokens * size,
        ),
    )(rows, cot, both, down, *kept, *first)


def lay_out_kernel(groups, member_ref, parts_ref, gate_ref, up_ref):
    member = member_ref[0]
    size = parts_ref.shape[2] // (2 * groups)
    for place in range(4):
        part = wide(parts_ref[jnp.bitwise_xor(place, member)])
        for half, out_ref in enumerate((gate_ref, up_ref)):
            for group in range(groups):
                start = (group * 4 + place) * size
                taken = (half * groups + group) * size
                out_ref[:, start : start + size] = part[:, taken : taken + size]


def lay_out(parts, member, groups):
    _, rows, columns = parts.shape
    return pl.pallas_call(
        functools.partial(lay_out_kernel, groups),
        out_shape=[jax.ShapeDtypeStruct((rows, 2 * columns), jnp.float32)] * 2,
        in_specs=[
            pl.BlockSpec(memory_space=pltpu.SMEM),
            pl.BlockSpec(memory_space=pltpu.VMEM),
        ],
        out_specs=[pl.BlockSpec(memory_space=pltpu.VMEM)] * 2,
        compiler_params=params(),
        cost_estimate=pl.CostEstimate(
            flops=0, bytes_accessed=24 * rows * columns, transcendentals=0
        ),
    )(member[None], parts)


def picked(value, groups, parts, part, first=0, size=None):
    whole = value.shape[1] // (groups * parts)
    size = whole if size is None else size
    row = lax.broadcasted_iota(jnp.int32, (value.shape[1], groups * size), 0)
    column = lax.broadcasted_iota(jnp.int32, (value.shape[1], groups * size), 1)
    wanted = (column // size * parts + part) * whole + first + column % size
    return narrow(times(value, (row == wanted).astype(value.dtype)))


def local(
    tokens,
    cotangent,
    in_weight,
    out_weight,
    gate_weight,
    up_weight,
    down_weight,
    mix_gain,
    ffn_gain,
    conv_taps,
):
    shards = lax.axis_size("shard")
    core = lax.axis_index("core")
    member = lax.axis_index("y") * 2 + core
    width = tokens.shape[-1]
    length = tokens.shape[1]
    half = width // 2
    own = mix_gain.shape[0]
    lane = half // shards

    small = jnp.concatenate([mix_gain[None], ffn_gain[None], conv_taps], 0)
    in_mine = jnp.concatenate(
        [picked(in_weight[:, i * width : (i + 1) * width], shards, 2, core) for i in range(3)], 1
    )
    out_rows = own // 2
    out_mine = lax.dynamic_slice(out_weight, (core * out_rows, 0), (out_rows, width))
    out_mine = jnp.concatenate([out_mine[:, :half], out_mine[:, half:]], 0)
    small_rows = jnp.pad(small, ((0, 11), (0, 4 * half - own)))
    mix_ring = Gather(
        jnp.concatenate([jnp.concatenate([in_mine, out_mine], 1), small_rows], 0), False
    )
    pair = jnp.concatenate([tokens[0], over_core(tokens[0])], 0)
    mix = mix_ring.end()

    quarter = down_weight.shape[0] // 4
    both = picked(jnp.concatenate([gate_weight, up_weight], 0), shards, 4, member)
    both_ring = Gather(jnp.concatenate([both[:own], both[own:]], 1), True)
    down_ring = Gather(
        lax.dynamic_slice(down_weight, (member * quarter, 0), (quarter, width)), False
    )
    both_full = flat(both_ring.end())
    down_full = flat(down_ring.end())

    small = wide(mix[:, own : own + 5, :own].transpose(1, 0, 2).reshape(5, width))
    gain_one, gain_two = small[0:1], small[1]
    taps = lax.dynamic_index_in_dim(
        small[2:5].reshape(3, shards, 2, lane), core, 2, keepdims=False
    ).reshape(3, half)

    normed, b_part, c_part, x_part, product = mix_in(pair, gain_one, mix, own)
    halo = lax.ppermute(
        product.reshape(2, length, half)[:, length - 2 :],
        "shard",
        [(i, i + 1) for i in range(shards - 1)],
    )
    conv, gated, branch = mix_out(c_part, product, halo, taps, mix, own)
    inputs = wide(tokens[0])
    resid = inputs + wide(branch[:length]) + wide(over_core(branch[length:]))

    factor_two = lax.rsqrt(jnp.mean(resid * resid, axis=-1, keepdims=True) + epsilon)
    unit_two = resid * factor_two
    hnorm = narrow(unit_two * gain_two)
    across = over_y(hnorm)
    hnorm_all = jnp.concatenate([hnorm, over_core(hnorm), across, over_core(across)], 0)
    cot = cotangent[0]
    cot_across = over_y(cot)
    cot_all = jnp.concatenate([cot, over_core(cot), cot_across, over_core(cot_across)], 0)

    hidden, d_both, d_far, out_far = feed_forward(hnorm_all, cot_all, both_full, down_full, 1)
    d_far = narrow(wide(over_core(d_far[length:])) + wide(d_far[:length]))
    hidden, d_both, d_near, out_near = feed_forward(
        hnorm_all, cot_all, both_full, down_full, 0, (hidden, d_both), (d_far,)
    )
    d_far = over_y(d_far)
    g_both = outer_sum(hnorm_all, d_both)
    g_down = outer_sum(hidden, cot_all)

    def rows_of(value):
        rows = value.shape[0] // shards
        return lambda place: lax.dynamic_slice(value, (place * rows, 0), (rows, value.shape[1]))

    back_both = Scatter(rows_of(g_both), True)
    back_down = Scatter(rows_of(g_down), False)
    d_near = wide(d_near[:length]) + wide(over_core(d_near[length:]))
    d_hnorm = d_near + wide(d_far)

    g_ffn_gain = jnp.sum(d_hnorm * unit_two, axis=0, keepdims=True)
    scaled_two = d_hnorm * gain_two
    d_resid = wide(cotangent[0]) + factor_two * (
        scaled_two - unit_two * jnp.mean(scaled_two * unit_two, axis=-1, keepdims=True)
    )
    out_far = tie(out_far, d_far)
    out_far = over_y(narrow(wide(over_core(out_far[length:])) + wide(out_far[:length])))
    out_near = wide(out_near[:length]) + wide(over_core(out_near[length:]))
    output = narrow(resid + out_near + wide(out_far))

    d_own = narrow(d_resid)
    d_branch = jnp.concatenate([d_own, over_core(d_own)], 0)
    d_c, d_product, edge, tap_grads = mix_back(
        d_branch, c_part, conv, product, halo, taps, mix, own
    )
    returned = lax.ppermute(edge, "shard", [(i + 1, i) for i in range(shards - 1)])
    g_out = outer_sum(gated, d_branch)
    d_mixed, d_normed, g_mix_gain = mix_last(
        d_product, returned, b_part, x_part, d_c, pair, mix, own
    )
    g_in = outer_sum(normed, d_mixed)
    spot = lax.broadcasted_iota(jnp.int32, (3, shards, 2, lane), 2)
    tap_full = jnp.where(spot == core, tap_grads.reshape(3, shards, 1, lane), 0.0)
    small_grads = jnp.concatenate([g_mix_gain, g_ffn_gain, tap_full.reshape(3, width)], 0)

    def mix_part(place):
        out = lax.dynamic_slice(g_out, (place * out_rows, 0), (out_rows, width))
        out = jnp.concatenate([out[:, :half], out[:, half:]], 0)
        main = lax.dynamic_slice(g_in, (place * own, 0), (own, 3 * half))
        few = lax.dynamic_slice(small_grads, (0, place * own), (5, own))
        few = jnp.pad(few, ((0, 11), (0, 4 * half - own)))
        return jnp.concatenate([jnp.concatenate([main, out], 1), few], 0)

    back_mix = Scatter(mix_part, False)
    d_normed = wide(d_normed[:length]) + wide(over_core(d_normed[length:]))
    factor_one = lax.rsqrt(jnp.mean(inputs * inputs, axis=-1, keepdims=True) + epsilon)
    unit_one = inputs * factor_one
    scaled_one = d_normed * gain_one
    d_inputs = d_resid + factor_one * (
        scaled_one - unit_one * jnp.mean(scaled_one * unit_one, axis=-1, keepdims=True)
    )

    def summed(value):
        return narrow(lax.psum(value, "outer") if lax.axis_size("outer") > 1 else value)

    def four_parts(value):
        mine = summed(value)
        across = over_y(mine)
        return jnp.stack([mine, over_core(mine), across, over_core(across)], 0)

    owned_gate, owned_up = lay_out(four_parts(back_both.end()), member, shards)
    down_parts = four_parts(back_down.end())
    owned_down = wide(
        jnp.concatenate(
            [
                lax.dynamic_index_in_dim(down_parts, jnp.bitwise_xor(i, member), 0, keepdims=False)
                for i in range(4)
            ],
            0,
        )
    )

    mix_mine = summed(back_mix.end())
    mix_mine = narrow(wide(mix_mine) + wide(over_y(mix_mine)))
    mix_other = over_core(mix_mine)
    low = jnp.where(core == 0, mix_mine, mix_other)
    high = jnp.where(core == 0, mix_other, mix_mine)
    owned_in = jnp.stack(
        [value[:own, : 3 * half].reshape(own, 3 * shards, lane) for value in (low, high)], 2
    )
    owned_in = wide(owned_in.reshape(own, 3 * width))
    owned_out = wide(
        jnp.concatenate(
            [
                jnp.concatenate([value[:out_rows, 3 * half :], value[out_rows:own, 3 * half :]], 1)
                for value in (low, high)
            ],
            0,
        )
    )
    small_owned = wide(low[own : own + 5, :own]) + wide(high[own : own + 5, :own])
    return (
        output[None],
        narrow(d_inputs)[None],
        owned_in,
        owned_out,
        owned_gate,
        owned_up,
        owned_down,
        small_owned[0],
        small_owned[1],
        small_owned[2:5],
    )


def solution(mesh):
    shards = mesh.shape["shard"]
    reps = mesh.shape["rep"]
    finer = Mesh(mesh.devices.reshape(shards, reps // 4, 2, 2), ("shard", "outer", "y", "core"))
    rep = ("outer", "y", "core")
    specs = (
        P(rep, "shard", None),
        P(rep, "shard", None),
        P("shard", None),
        P("shard", None),
        P("shard", None),
        P("shard", None),
        P("shard", None),
        P("shard"),
        P("shard"),
        P(None, "shard"),
    )
    return jax.shard_map(local, mesh=finer, in_specs=specs, out_specs=specs, check_vma=False)
```

```python
import functools

import jax
import jax.numpy as jnp
from jax import lax
from jax.experimental import pallas as pl
from jax.experimental.pallas import tpu as pltpu
from jax.sharding import Mesh, PartitionSpec as P

epsilon = 1e-05
PAIR = ((0, 1), (1, 0))
FIRST = 2
AFTER = 0
BACK = 1


def over_core(value):
    return lax.ppermute(value, "core", PAIR)


def over_y(value):
    return lax.ppermute(value, "y", PAIR)


def outer_sum(left, right):
    return lax.dot_general(
        left, right, (((0,), (0,)), ((), ())), preferred_element_type=jnp.float32
    )


def times_transposed(grad, weight):
    return lax.dot_general(
        grad, weight, (((1,), (1,)), ((), ())), preferred_element_type=jnp.float32
    )


def times(value, weight):
    return jnp.dot(value, weight, preferred_element_type=jnp.float32)


def wide(value):
    return value.astype(jnp.float32)


def narrow(value):
    return value.astype(jnp.bfloat16)


def tie_kernel(*refs):
    del refs


def tie(value, *others):
    return pl.pallas_call(
        tie_kernel,
        out_shape=jax.ShapeDtypeStruct(value.shape, value.dtype),
        in_specs=[pl.BlockSpec(memory_space=pl.ANY)] * (1 + len(others)),
        out_specs=pl.BlockSpec(memory_space=pl.ANY),
        input_output_aliases={0: 0},
    )(value, *others)


def ring_order(count):
    return list(range(0, count, 2)) + list(range(1, count, 2))[::-1]


def ring_pairs(count):
    order = ring_order(count)
    ahead = [(order[i], order[(i + 1) % count]) for i in range(count)]
    return ahead, [(b, a) for a, b in ahead]


def ring_place(count, offset):
    me = lax.axis_index("shard")
    here = jnp.where(me % 2 == 0, me // 2, count - 1 - me // 2)
    there = (here + offset) % count
    return jnp.where(there < count // 2, 2 * there, 2 * (count - 1 - there) + 1)


class Gather:
    def __init__(self, block, flip):
        self.count = lax.axis_size("shard")
        self.far, self.near = self.count // 2, self.count - 1 - self.count // 2
        self.sign = -1 if flip else 1
        self.pairs = ring_pairs(self.count)[:: self.sign]
        self.step = 0
        self.one = self.two = block
        self.whole = jnp.zeros((self.count,) + block.shape, block.dtype)
        self.put(block, 0)

    def put(self, block, offset):
        place = ring_place(self.count, offset)
        self.whole = lax.dynamic_update_slice(self.whole, block[None], (place, 0, 0))

    def hop(self):
        self.step += 1
        if self.step <= self.far:
            self.one = lax.ppermute(self.one, "shard", self.pairs[0])
            self.put(self.one, -self.sign * self.step)
        if self.step <= self.near:
            self.two = lax.ppermute(self.two, "shard", self.pairs[1])
            self.put(self.two, self.sign * self.step)
        return self

    def end(self):
        while self.step < self.far:
            self.hop()
        return self.whole


class Scatter:
    def __init__(self, part, flip):
        self.count = lax.axis_size("shard")
        self.far, self.near = self.count // 2, self.count - 1 - self.count // 2
        self.sign = -1 if flip else 1
        self.pairs = ring_pairs(self.count)[:: self.sign]
        self.step = 0
        self.part = lambda offset: wide(part(ring_place(self.count, offset)))
        self.one = narrow(self.part(self.sign * self.far))
        self.two = narrow(self.part(-self.sign * self.near))

    def hop(self):
        self.step += 1
        if self.step <= self.far:
            self.one = lax.ppermute(self.one, "shard", self.pairs[0])
            if self.step < self.far:
                self.one = narrow(wide(self.one) + self.part(self.sign * (self.far - self.step)))
        if self.step <= self.near:
            self.two = lax.ppermute(self.two, "shard", self.pairs[1])
            if self.step < self.near:
                self.two = narrow(wide(self.two) + self.part(-self.sign * (self.near - self.step)))
        return self

    def end(self):
        while self.step < self.far:
            self.hop()
        return self.part(0) + wide(self.one) + wide(self.two)


def rows_block(tile, columns, first=0):
    return pl.BlockSpec((tile, columns), lambda i: (first + i, 0))


def whole_block(shape):
    zeros = (0,) * len(shape)
    return pl.BlockSpec(shape, lambda i: zeros, pipeline_mode=pl.Buffered(1))


def params(size=48):
    return pltpu.CompilerParams(vmem_limit_bytes=size * 2**20)


def flat(value):
    return value.reshape(-1, value.shape[-1])


def mix_in_kernel(half, own, tokens_ref, gain_ref, mix_ref, normed_ref, b_ref, c_ref, x_ref, p_ref):
    inputs = wide(tokens_ref[...])
    unit = inputs * lax.rsqrt(jnp.mean(inputs * inputs, axis=-1, keepdims=True) + epsilon)
    normed = narrow(unit * gain_ref[...])
    normed_ref[...] = normed
    for i, ref in enumerate((b_ref, c_ref, x_ref)):
        ref[...] = times(normed, flat(mix_ref[:, :own, i * half : (i + 1) * half]))
    p_ref[...] = narrow(b_ref[...] * x_ref[...])


def mix_in(tokens, gain, mix, own):
    count, width = tokens.shape
    half = width // 4
    tile = count // 4
    f32, bf16 = jnp.float32, jnp.bfloat16
    shapes = [(width, bf16), (half, f32), (half, f32), (half, f32), (half, bf16)]
    return pl.pallas_call(
        functools.partial(mix_in_kernel, half, own),
        grid=(4,),
        in_specs=[rows_block(tile, width), whole_block((1, width)), whole_block(mix.shape)],
        out_specs=[rows_block(tile, columns) for columns, _ in shapes],
        out_shape=[jax.ShapeDtypeStruct((count, columns), kind) for columns, kind in shapes],
        compiler_params=params(),
        cost_estimate=pl.CostEstimate(
            flops=6 * count * width * half, bytes_accessed=14 * count * width, transcendentals=0
        ),
    )(tokens, gain, mix)


def delayed(product, halo):
    row = lax.broadcasted_iota(jnp.int32, product.shape, 0)
    one = jnp.where(row == 0, halo[1:2], pltpu.roll(product, 1, 0))
    two = jnp.where(row == 0, halo[0:1], jnp.where(row == 1, halo[1:2], pltpu.roll(product, 2, 0)))
    return one, two


def mix_out_kernel(half, own, c_ref, p_ref, halo_ref, taps_ref, mix_ref, conv_ref, gated_ref, out_ref):
    product = wide(p_ref[...])
    one, two = delayed(product, wide(halo_ref[0]))
    conv = taps_ref[0:1] * two + taps_ref[1:2] * one + taps_ref[2:3] * product
    conv_ref[...] = conv
    gated = narrow(c_ref[...] * conv)
    gated_ref[...] = gated
    for i in range(4):
        weight = flat(mix_ref[:, i * own // 4 : (i + 1) * own // 4, 3 * half :])
        out_ref[:, i * half : (i + 1) * half] = narrow(times(gated, weight))


def mix_out(c_part, product, halo, taps, mix, own):
    count, half = product.shape
    length = count // 4
    shapes = [(half, jnp.float32), (half, jnp.bfloat16), (4 * half, jnp.bfloat16)]
    return pl.pallas_call(
        functools.partial(mix_out_kernel, half, own),
        grid=(4,),
        in_specs=[
            rows_block(length, half),
            rows_block(length, half),
            pl.BlockSpec((1,) + halo.shape[1:], lambda i: (i, 0, 0)),
            whole_block(taps.shape),
            whole_block(mix.shape),
        ],
        out_specs=[rows_block(length, columns) for columns, _ in shapes],
        out_shape=[jax.ShapeDtypeStruct((count, columns), kind) for columns, kind in shapes],
        compiler_params=params(),
        cost_estimate=pl.CostEstimate(
            flops=4 * count * half * half, bytes_accessed=16 * count * half, transcendentals=0
        ),
    )(c_part, product, halo, taps, mix)


def mix_back_kernel(
    half, own, d_ref, c_ref, conv_ref, p_ref, halo_ref, taps_ref, mix_ref, d_c_ref, d_p_ref, edge_ref, sums_ref
):
    grad = d_ref[...]
    d_gated = sum(
        times_transposed(
            grad[:, i * half : (i + 1) * half],
            flat(mix_ref[:, i * own // 4 : (i + 1) * own // 4, 3 * half :]),
        )
        for i in range(4)
    )
    d_c_ref[...] = narrow(d_gated * conv_ref[...])
    d_conv = d_gated * c_ref[...]
    product = wide(p_ref[...])
    one, two = delayed(product, wide(halo_ref[0]))

    @pl.when(pl.program_id(0) == 0)
    def _():
        sums_ref[...] = jnp.zeros_like(sums_ref)

    for k, value in enumerate((two, one, product)):
        sums_ref[k : k + 1] += jnp.sum(d_conv * value, axis=0, keepdims=True)
    taps = taps_ref[...]
    length = d_conv.shape[0]
    row = lax.broadcasted_iota(jnp.int32, d_conv.shape, 0)
    later = jnp.where(row < length - 1, pltpu.roll(d_conv, length - 1, 0), 0.0)
    latest = jnp.where(row < length - 2, pltpu.roll(d_conv, length - 2, 0), 0.0)
    d_p_ref[...] = taps[2:3] * d_conv + taps[1:2] * later + taps[0:1] * latest
    edge_ref[0, 0:1] = taps[0:1] * d_conv[0:1]
    edge_ref[0, 1:2] = taps[0:1] * d_conv[1:2] + taps[1:2] * d_conv[0:1]


def mix_back(d_branch, c_part, conv, product, halo, taps, mix, own):
    count, half = product.shape
    length = count // 4
    f32 = jnp.float32
    return pl.pallas_call(
        functools.partial(mix_back_kernel, half, own),
        grid=(4,),
        in_specs=[
            rows_block(length, 4 * half),
            rows_block(length, half),
            rows_block(length, half),
            rows_block(length, half),
            pl.BlockSpec((1,) + halo.shape[1:], lambda i: (i, 0, 0)),
            whole_block(taps.shape),
            whole_block(mix.shape),
        ],
        out_specs=[
            rows_block(length, half),
            rows_block(length, half),
            pl.BlockSpec((1, 2, half), lambda i: (i, 0, 0)),
            pl.BlockSpec((3, half), lambda i: (0, 0)),
        ],
        out_shape=[
            jax.ShapeDtypeStruct((count, half), jnp.bfloat16),
            jax.ShapeDtypeStruct((count, half), f32),
            jax.ShapeDtypeStruct((4, 2, half), f32),
            jax.ShapeDtypeStruct((3, half), f32),
        ],
        compiler_params=params(),
        cost_estimate=pl.CostEstimate(
            flops=4 * count * half * half // 10, bytes_accessed=2 * count * half, transcendentals=0
        ),
    )(d_branch, c_part, conv, product, halo, taps, mix)


def mix_last_kernel(
    half, own, d_p_ref, edge_ref, b_ref, x_ref, d_c_ref, tokens_ref, mix_ref, d_mixed_ref, d_n_ref, sums_ref
):
    d_product = d_p_ref[...]
    length = d_product.shape[0]
    row = lax.broadcasted_iota(jnp.int32, d_product.shape, 0)
    edge = edge_ref[0]
    d_product += jnp.where(
        row == length - 2, edge[0:1], jnp.where(row == length - 1, edge[1:2], 0.0)
    )
    d_mixed_ref[:, :half] = narrow(d_product * x_ref[...])
    d_mixed_ref[:, half : 2 * half] = d_c_ref[...]
    d_mixed_ref[:, 2 * half :] = narrow(d_product * b_ref[...])
    d_normed = times_transposed(d_mixed_ref[...], flat(mix_ref[:, :own, : 3 * half]))
    d_n_ref[...] = narrow(d_normed)
    inputs = wide(tokens_ref[...])
    unit = inputs * lax.rsqrt(jnp.mean(inputs * inputs, axis=-1, keepdims=True) + epsilon)

    @pl.when(pl.program_id(0) == 0)
    def _():
        sums_ref[...] = jnp.zeros_like(sums_ref)

    sums_ref[...] += jnp.sum(d_normed * unit, axis=0, keepdims=True)


def mix_last(d_product, edge, b_part, x_part, d_c, tokens, mix, own):
    count, half = d_product.shape
    length = count // 4
    return pl.pallas_call(
        functools.partial(mix_last_kernel, half, own),
        grid=(4,),
        in_specs=[
            rows_block(length, half),
            pl.BlockSpec((1, 2, half), lambda i: (i, 0, 0)),
            rows_block(length, half),
            rows_block(length, half),
            rows_block(length, half),
            rows_block(length, 4 * half),
            whole_block(mix.shape),
        ],
        out_specs=[
            rows_block(length, 3 * half),
            rows_block(length, 4 * half),
            pl.BlockSpec((1, 4 * half), lambda i: (0, 0)),
        ],
        out_shape=[
            jax.ShapeDtypeStruct((count, 3 * half), jnp.bfloat16),
            jax.ShapeDtypeStruct((count, 4 * half), jnp.bfloat16),
            jax.ShapeDtypeStruct((1, 4 * half), jnp.float32),
        ],
        compiler_params=params(),
        cost_estimate=pl.CostEstimate(
            flops=12 * count * half * half // 10, bytes_accessed=2 * count * half, transcendentals=0
        ),
    )(d_product, edge, b_part, x_part, d_c, tokens, mix)


def feed_forward_kernel(size, top, rows_ref, cot_ref, chunk_ref, *refs):
    hidden_ref, d_both_ref, d_rows_ref, out_ref = refs[-4:]
    rows = rows_ref[...]
    cot = cot_ref[...]
    down = flat(chunk_ref[:, 2 * top :, : rows.shape[1]])
    for start in range(0, size, 256):
        stop = min(start + 256, size)
        gate = times(rows, flat(chunk_ref[:, :top, start:stop]))
        upper = times(rows, flat(chunk_ref[:, top : 2 * top, start:stop]))
        d_hidden = times_transposed(cot, down[start:stop])
        sigma = jax.nn.sigmoid(gate)
        activated = gate * sigma
        hidden_ref[:, start:stop] = narrow(activated * upper)
        d_both_ref[:, start:stop] = narrow(d_hidden * upper * sigma * (1.0 + gate * (1.0 - sigma)))
        d_both_ref[:, size + start : size + stop] = narrow(d_hidden * activated)
    d_rows = times_transposed(d_both_ref[:, :size], flat(chunk_ref[:, :top]))
    d_rows += times_transposed(d_both_ref[:, size:], flat(chunk_ref[:, top : 2 * top]))
    d_rows_ref[...] = narrow(d_rows)
    out_ref[...] = narrow(times(hidden_ref[...], down))


def feed_forward(rows, cot, chunk, at, kept=(), first=()):
    width = rows.shape[1]
    tokens = cot.shape[0] // 2
    tile = tokens // 2
    size = chunk.shape[2]
    here = 2 * at
    aliases = {3 + i: i for i in range(len(kept))}
    return pl.pallas_call(
        functools.partial(feed_forward_kernel, size, width // chunk.shape[0]),
        grid=(2,),
        in_specs=[
            rows_block(tile, width, here if rows.shape[0] > tokens else 0),
            rows_block(tile, width, here),
            whole_block(chunk.shape),
        ]
        + [pl.BlockSpec(memory_space=pl.ANY)] * (len(kept) + len(first)),
        out_specs=[
            rows_block(tile, size, here),
            rows_block(tile, 2 * size, here),
            rows_block(tile, width),
            rows_block(tile, width),
        ],
        out_shape=[
            jax.ShapeDtypeStruct((2 * tokens, size), jnp.bfloat16),
            jax.ShapeDtypeStruct((2 * tokens, 2 * size), jnp.bfloat16),
            jax.ShapeDtypeStruct((tokens, width), jnp.bfloat16),
            jax.ShapeDtypeStruct((tokens, width), jnp.bfloat16),
        ],
        input_output_aliases=aliases,
        compiler_params=params(),
        cost_estimate=pl.CostEstimate(
            flops=12 * tokens * width * size,
            bytes_accessed=16 * tokens * width,
            transcendentals=tokens * size,
        ),
    )(rows, cot, chunk, *kept, *first)


def lay_out_kernel(groups, member_ref, parts_ref, gate_ref, up_ref, down_ref):
    member = member_ref[0]
    size = parts_ref.shape[2] // groups
    rows = gate_ref.shape[0]
    for place in range(4):
        part = wide(parts_ref[jnp.bitwise_xor(place, member)])
        for half, out_ref in enumerate((gate_ref, up_ref)):
            for group in range(groups):
                start = (group * 4 + place) * size
                out_ref[:, start : start + size] = part[
                    half * rows : (half + 1) * rows, group * size : (group + 1) * size
                ]
        down_ref[place * size : (place + 1) * size, :] = part[2 * rows :, : down_ref.shape[1]]


def lay_out(parts, member, groups, rows, width):
    columns = parts.shape[2]
    shapes = [(rows, 4 * columns), (rows, 4 * columns), (4 * columns // groups, width)]
    return pl.pallas_call(
        functools.partial(lay_out_kernel, groups),
        out_shape=[jax.ShapeDtypeStruct(shape, jnp.float32) for shape in shapes],
        in_specs=[
            pl.BlockSpec(memory_space=pltpu.SMEM),
            pl.BlockSpec(memory_space=pltpu.VMEM),
        ],
        out_specs=[pl.BlockSpec(memory_space=pltpu.VMEM)] * 3,
        compiler_params=params(),
        cost_estimate=pl.CostEstimate(
            flops=0, bytes_accessed=72 * rows * columns, transcendentals=0
        ),
    )(member[None], parts)


def lay_out_mix_kernel(groups, own, member_ref, parts_ref, in_ref, out_ref, small_ref):
    member = member_ref[0]
    part_size = parts_ref.shape[2] // 4
    lane = part_size // groups
    rows = own // 4
    for place in range(4):
        part = wide(parts_ref[jnp.bitwise_xor(place, member)])
        for group in range(3 * groups):
            start = (group * 4 + place) * lane
            in_ref[:, start : start + lane] = part[:own, group * lane : (group + 1) * lane]
        for i in range(4):
            out_ref[place * rows : (place + 1) * rows, i * part_size : (i + 1) * part_size] = part[
                i * rows : (i + 1) * rows, 3 * part_size :
            ]
    few = [wide(parts_ref[i])[own:, :own] for i in range(4)]
    small_ref[...] = (few[0] + few[1]) + (few[2] + few[3])


def lay_out_mix(parts, member, groups, own):
    width = parts.shape[2]
    shapes = [(own, 3 * width), (own, width), (parts.shape[1] - own, own)]
    return pl.pallas_call(
        functools.partial(lay_out_mix_kernel, groups, own),
        out_shape=[jax.ShapeDtypeStruct(shape, jnp.float32) for shape in shapes],
        in_specs=[
            pl.BlockSpec(memory_space=pltpu.SMEM),
            pl.BlockSpec(memory_space=pltpu.VMEM),
        ],
        out_specs=[pl.BlockSpec(memory_space=pltpu.VMEM)] * 3,
        compiler_params=params(),
        cost_estimate=pl.CostEstimate(flops=0, bytes_accessed=24 * own * width, transcendentals=0),
    )(member[None], parts)


def four_gather(value):
    across = over_y(value)
    return jnp.concatenate([value, over_core(value), across, over_core(across)], 0)


def far_sum(value):
    rows = value.shape[0] // 4
    return narrow(wide(over_core(value[3 * rows :])) + wide(value[2 * rows : 3 * rows]))


def near_sum(value):
    rows = value.shape[0] // 4
    return wide(value[:rows]) + wide(over_core(value[rows : 2 * rows]))


def picked(value, groups, parts, part, first=0, size=None):
    whole = value.shape[1] // (groups * parts)
    size = whole if size is None else size
    row = lax.broadcasted_iota(jnp.int32, (value.shape[1], groups * size), 0)
    column = lax.broadcasted_iota(jnp.int32, (value.shape[1], groups * size), 1)
    wanted = (column // size * parts + part) * whole + first + column % size
    return narrow(times(value, (row == wanted).astype(value.dtype)))


def local(
    tokens,
    cotangent,
    in_weight,
    out_weight,
    gate_weight,
    up_weight,
    down_weight,
    mix_gain,
    ffn_gain,
    conv_taps,
):
    shards = lax.axis_size("shard")
    core = lax.axis_index("core")
    member = lax.axis_index("y") * 2 + core
    width = tokens.shape[-1]
    length = tokens.shape[1]
    half = width // 4
    own = mix_gain.shape[0]
    lane = half // shards

    small = jnp.concatenate([mix_gain[None], ffn_gain[None], conv_taps], 0)
    in_mine = jnp.concatenate(
        [picked(in_weight[:, i * width : (i + 1) * width], shards, 4, member) for i in range(3)], 1
    )
    out_rows = own // 4
    out_mine = lax.dynamic_slice(out_weight, (member * out_rows, 0), (out_rows, width))
    out_mine = jnp.concatenate([out_mine[:, i * half : (i + 1) * half] for i in range(4)], 0)
    small_rows = jnp.pad(small, ((0, 11), (0, 4 * half - own)))
    mix_ring = Gather(
        jnp.concatenate([jnp.concatenate([in_mine, out_mine], 1), small_rows], 0), False
    )
    tokens_across = over_y(tokens[0])
    mix_ring.hop()

    quarter = down_weight.shape[0] // 4
    size = shards * quarter
    both = jnp.concatenate([gate_weight, up_weight], 0)
    if FIRST == 1:
        both = tie(both, mix_ring.one, mix_ring.two)
    both = picked(both, shards, 4, member)
    down = lax.dynamic_slice(down_weight, (member * quarter, 0), (quarter, width))
    block = jnp.concatenate([both, jnp.pad(down, ((0, 0), (0, size - width)))], 0)
    mix_ring.hop()
    mix_ring.one = tie(mix_ring.one, tokens_across)
    if FIRST == 2:
        block = tie(block, mix_ring.one, mix_ring.two)
    mix_ring.hop()
    if FIRST == 3:
        block = tie(block, mix_ring.one, mix_ring.two)
    mix = mix_ring.end()
    pair = jnp.concatenate(
        [tokens[0], over_core(tokens[0]), tokens_across, over_core(tokens_across)], 0
    )
    ring = Gather(block, True)
    ring.hop()
    ring.hop()

    small = wide(mix[:, own : own + 5, :own].transpose(1, 0, 2).reshape(5, width))
    gain_one, gain_two = small[0:1], small[1]
    taps = lax.dynamic_index_in_dim(
        small[2:5].reshape(3, shards, 4, lane), member, 2, keepdims=False
    ).reshape(3, half)

    normed, b_part, c_part, x_part, product = mix_in(pair, gain_one, mix, own)
    halo = lax.ppermute(
        product.reshape(4, length, half)[:, length - 2 :],
        "shard",
        [(i, i + 1) for i in range(shards - 1)],
    )
    conv, gated, branch = mix_out(c_part, product, halo, taps, mix, own)
    inputs = wide(tokens[0])
    resid = inputs + near_sum(branch) + wide(over_y(far_sum(branch)))

    factor_two = lax.rsqrt(jnp.mean(resid * resid, axis=-1, keepdims=True) + epsilon)
    unit_two = resid * factor_two
    hnorm = narrow(unit_two * gain_two)
    if AFTER:
        ring.one, ring.two = tie(ring.one, hnorm), tie(ring.two, hnorm)
    chunk = ring.end()
    if quarter % 16:
        chunk = jnp.concatenate(
            [flat(chunk[:, :own]), flat(chunk[:, own : 2 * own]), flat(chunk[:, 2 * own :])], 0
        )[None]
    across = over_y(hnorm)
    hnorm_near = jnp.concatenate([hnorm, over_core(hnorm)], 0)
    cot = cotangent[0]
    cot_across = over_y(cot)
    cot_all = jnp.concatenate([cot, over_core(cot), cot_across, over_core(cot_across)], 0)

    hidden, d_both, d_near, out_near = feed_forward(hnorm_near, cot_all, chunk, 0)
    across = tie(across, hidden)
    hnorm_all = jnp.concatenate([hnorm_near, across, over_core(across)], 0)
    hidden, d_both, d_far, out_far = feed_forward(hnorm_all, cot_all, chunk, 1, (hidden, d_both))
    g_down = outer_sum(hidden, cot_all)
    d_far = narrow(wide(over_core(d_far[length:])) + wide(d_far[:length]))
    d_both = tie(d_both, d_far)
    d_far = over_y(d_far)
    g_both = outer_sum(hnorm_all, d_both)

    def part(place):
        both = lax.dynamic_slice(g_both, (place * own, 0), (own, 2 * size))
        down = lax.dynamic_slice(g_down, (place * quarter, 0), (quarter, width))
        down = jnp.pad(down, ((0, 0), (0, size - width)))
        return jnp.concatenate([both[:, :size], both[:, size:], down], 0)

    back = Scatter(part, True)
    back.hop()
    d_near = wide(d_near[:length]) + wide(over_core(d_near[length:]))
    d_hnorm = d_near + wide(d_far)

    g_ffn_gain = jnp.sum(d_hnorm * unit_two, axis=0, keepdims=True)
    scaled_two = d_hnorm * gain_two
    d_resid = wide(cotangent[0]) + factor_two * (
        scaled_two - unit_two * jnp.mean(scaled_two * unit_two, axis=-1, keepdims=True)
    )
    d_own = narrow(d_resid)
    back.one, back.two = tie(back.one, d_own), tie(back.two, d_own)
    back.hop()
    d_branch = four_gather(d_own)
    back.one, back.two = tie(back.one, d_branch), tie(back.two, d_branch)
    back.hop()
    d_c, d_product, edge, tap_grads = mix_back(
        d_branch, c_part, conv, product, halo, taps, mix, own
    )
    returned = lax.ppermute(edge, "shard", [(i + 1, i) for i in range(shards - 1)])
    g_out = outer_sum(gated, d_branch)
    d_mixed, d_normed, g_mix_gain = mix_last(
        d_product, returned, b_part, x_part, d_c, pair, mix, own
    )
    g_in = outer_sum(normed, tie(d_mixed, back.one, back.two))
    spot = lax.broadcasted_iota(jnp.int32, (3, shards, 4, lane), 2)
    tap_full = jnp.where(spot == member, tap_grads.reshape(3, shards, 1, lane), 0.0)
    small_grads = jnp.concatenate([g_mix_gain, g_ffn_gain, tap_full.reshape(3, width)], 0)

    def mix_part(place):
        out = lax.dynamic_slice(g_out, (place * out_rows, 0), (out_rows, width))
        out = jnp.concatenate([out[:, i * half : (i + 1) * half] for i in range(4)], 0)
        main = lax.dynamic_slice(g_in, (place * own, 0), (own, 3 * half))
        few = lax.dynamic_slice(small_grads, (0, place * own), (5, own))
        few = jnp.pad(few, ((0, 11), (0, 4 * half - own)))
        return jnp.concatenate([jnp.concatenate([main, out], 1), few], 0)

    back_mix = Scatter(mix_part, False)
    back.hop()
    back_mix.hop()
    out_far = narrow(wide(over_core(out_far[length:])) + wide(out_far[:length]))
    out_far = over_y(tie(out_far, d_far))
    out_near = wide(out_near[:length]) + wide(over_core(out_near[length:]))
    if BACK == 1:
        back_mix.one = tie(back_mix.one, out_far)
    if BACK == 2:
        back_mix.one = tie(back_mix.one, out_far, back.one)
    back_mix.hop()
    output = narrow(tie(resid, back_mix.one) + out_near + wide(out_far))
    d_normed_far = over_y(tie(far_sum(d_normed), out_far))
    back_mix.one = tie(back_mix.one, d_normed_far)
    d_normed = near_sum(d_normed) + wide(d_normed_far)
    factor_one = lax.rsqrt(jnp.mean(inputs * inputs, axis=-1, keepdims=True) + epsilon)
    unit_one = inputs * factor_one
    scaled_one = d_normed * gain_one
    d_inputs = d_resid + factor_one * (
        scaled_one - unit_one * jnp.mean(scaled_one * unit_one, axis=-1, keepdims=True)
    )

    def summed(value):
        return narrow(lax.psum(value, "outer") if lax.axis_size("outer") > 1 else value)

    def four_parts(value):
        mine = summed(value)
        across = over_y(mine)
        return jnp.stack([mine, over_core(mine), across, over_core(across)], 0)

    owned_gate, owned_up, owned_down = lay_out(
        four_parts(back.end()), member, shards, own, width
    )

    owned_in, owned_out, small_owned = lay_out_mix(
        four_parts(back_mix.end()), member, shards, own
    )
    return (
        output[None],
        narrow(d_inputs)[None],
        owned_in,
        owned_out,
        owned_gate,
        owned_up,
        owned_down,
        small_owned[0],
        small_owned[1],
        small_owned[2:5],
    )


def solution(mesh):
    shards = mesh.shape["shard"]
    reps = mesh.shape["rep"]
    finer = Mesh(mesh.devices.reshape(shards, reps // 4, 2, 2), ("shard", "outer", "y", "core"))
    rep = ("outer", "y", "core")
    specs = (
        P(rep, "shard", None),
        P(rep, "shard", None),
        P("shard", None),
        P("shard", None),
        P("shard", None),
        P("shard", None),
        P("shard", None),
        P("shard"),
        P("shard"),
        P(None, "shard"),
    )
    return jax.shard_map(local, mesh=finer, in_specs=specs, out_specs=specs, check_vma=False)
```

```python
import functools

import jax
import jax.numpy as jnp
from jax import lax
from jax.experimental import pallas as pl
from jax.experimental.pallas import tpu as pltpu
from jax.sharding import Mesh, PartitionSpec as P

epsilon = 1e-05
PAIR = ((0, 1), (1, 0))
FIRST = 2
AFTER = 0
BACK = 1


def over_core(value):
    return lax.ppermute(value, "core", PAIR)


def over_y(value):
    return lax.ppermute(value, "y", PAIR)


def outer_sum(left, right):
    return lax.dot_general(
        left, right, (((0,), (0,)), ((), ())), preferred_element_type=jnp.float32
    )


def times_transposed(grad, weight):
    return lax.dot_general(
        grad, weight, (((1,), (1,)), ((), ())), preferred_element_type=jnp.float32
    )


def times(value, weight):
    return jnp.dot(value, weight, preferred_element_type=jnp.float32)


def wide(value):
    return value.astype(jnp.float32)


def narrow(value):
    return value.astype(jnp.bfloat16)


def tie_kernel(*refs):
    del refs


def tie(value, *others):
    return pl.pallas_call(
        tie_kernel,
        out_shape=jax.ShapeDtypeStruct(value.shape, value.dtype),
        in_specs=[pl.BlockSpec(memory_space=pl.ANY)] * (1 + len(others)),
        out_specs=pl.BlockSpec(memory_space=pl.ANY),
        input_output_aliases={0: 0},
    )(value, *others)


def ring_order(count):
    return list(range(0, count, 2)) + list(range(1, count, 2))[::-1]


def ring_pairs(count):
    order = ring_order(count)
    ahead = [(order[i], order[(i + 1) % count]) for i in range(count)]
    return ahead, [(b, a) for a, b in ahead]


def ring_place(count, offset):
    me = lax.axis_index("shard")
    here = jnp.where(me % 2 == 0, me // 2, count - 1 - me // 2)
    there = (here + offset) % count
    return jnp.where(there < count // 2, 2 * there, 2 * (count - 1 - there) + 1)


class Gather:
    def __init__(self, block, flip):
        self.count = lax.axis_size("shard")
        self.far, self.near = self.count // 2, self.count - 1 - self.count // 2
        self.sign = -1 if flip else 1
        self.pairs = ring_pairs(self.count)[:: self.sign]
        self.step = 0
        self.one = self.two = block
        self.whole = jnp.zeros((self.count,) + block.shape, block.dtype)
        self.put(block, 0)

    def put(self, block, offset):
        place = ring_place(self.count, offset)
        self.whole = lax.dynamic_update_slice(self.whole, block[None], (place, 0, 0))

    def hop(self):
        self.step += 1
        if self.step <= self.far:
            self.one = lax.ppermute(self.one, "shard", self.pairs[0])
            self.put(self.one, -self.sign * self.step)
        if self.step <= self.near:
            self.two = lax.ppermute(self.two, "shard", self.pairs[1])
            self.put(self.two, self.sign * self.step)
        return self

    def end(self):
        while self.step < self.far:
            self.hop()
        return self.whole


class Scatter:
    def __init__(self, part, flip):
        self.count = lax.axis_size("shard")
        self.far, self.near = self.count // 2, self.count - 1 - self.count // 2
        self.sign = -1 if flip else 1
        self.pairs = ring_pairs(self.count)[:: self.sign]
        self.step = 0
        self.part = lambda offset: wide(part(ring_place(self.count, offset)))
        self.one = narrow(self.part(self.sign * self.far))
        self.two = narrow(self.part(-self.sign * self.near))

    def hop(self):
        self.step += 1
        if self.step <= self.far:
            self.one = lax.ppermute(self.one, "shard", self.pairs[0])
            if self.step < self.far:
                self.one = narrow(wide(self.one) + self.part(self.sign * (self.far - self.step)))
        if self.step <= self.near:
            self.two = lax.ppermute(self.two, "shard", self.pairs[1])
            if self.step < self.near:
                self.two = narrow(wide(self.two) + self.part(-self.sign * (self.near - self.step)))
        return self

    def end(self):
        while self.step < self.far:
            self.hop()
        return self.part(0) + wide(self.one) + wide(self.two)


def rows_block(tile, columns, first=0):
    return pl.BlockSpec((tile, columns), lambda i: (first + i, 0))


def whole_block(shape):
    zeros = (0,) * len(shape)
    return pl.BlockSpec(shape, lambda i: zeros, pipeline_mode=pl.Buffered(1))


def params(size=48):
    return pltpu.CompilerParams(vmem_limit_bytes=size * 2**20)


def flat(value):
    return value.reshape(-1, value.shape[-1])


def mix_in_kernel(half, own, tokens_ref, gain_ref, mix_ref, normed_ref, b_ref, c_ref, x_ref, p_ref):
    inputs = wide(tokens_ref[...])
    unit = inputs * lax.rsqrt(jnp.mean(inputs * inputs, axis=-1, keepdims=True) + epsilon)
    normed = narrow(unit * gain_ref[...])
    normed_ref[...] = normed
    for i, ref in enumerate((b_ref, c_ref, x_ref)):
        ref[...] = times(normed, flat(mix_ref[:, :own, i * half : (i + 1) * half]))
    p_ref[...] = narrow(b_ref[...] * x_ref[...])


def mix_in(tokens, gain, mix, own):
    count, width = tokens.shape
    half = width // 4
    tile = count // 4
    f32, bf16 = jnp.float32, jnp.bfloat16
    shapes = [(width, bf16), (half, f32), (half, f32), (half, f32), (half, bf16)]
    return pl.pallas_call(
        functools.partial(mix_in_kernel, half, own),
        grid=(4,),
        in_specs=[rows_block(tile, width), whole_block((1, width)), whole_block(mix.shape)],
        out_specs=[rows_block(tile, columns) for columns, _ in shapes],
        out_shape=[jax.ShapeDtypeStruct((count, columns), kind) for columns, kind in shapes],
        compiler_params=params(),
        cost_estimate=pl.CostEstimate(
            flops=6 * count * width * half, bytes_accessed=14 * count * width, transcendentals=0
        ),
    )(tokens, gain, mix)


def delayed(product, halo):
    row = lax.broadcasted_iota(jnp.int32, product.shape, 0)
    one = jnp.where(row == 0, halo[1:2], pltpu.roll(product, 1, 0))
    two = jnp.where(row == 0, halo[0:1], jnp.where(row == 1, halo[1:2], pltpu.roll(product, 2, 0)))
    return one, two


def mix_out_kernel(half, own, c_ref, p_ref, halo_ref, taps_ref, mix_ref, conv_ref, gated_ref, out_ref):
    product = wide(p_ref[...])
    one, two = delayed(product, wide(halo_ref[0]))
    conv = taps_ref[0:1] * two + taps_ref[1:2] * one + taps_ref[2:3] * product
    conv_ref[...] = conv
    gated = narrow(c_ref[...] * conv)
    gated_ref[...] = gated
    for i in range(4):
        weight = flat(mix_ref[:, i * own // 4 : (i + 1) * own // 4, 3 * half :])
        out_ref[:, i * half : (i + 1) * half] = narrow(times(gated, weight))


def mix_out(c_part, product, halo, taps, mix, own):
    count, half = product.shape
    length = count // 4
    shapes = [(half, jnp.float32), (half, jnp.bfloat16), (4 * half, jnp.bfloat16)]
    return pl.pallas_call(
        functools.partial(mix_out_kernel, half, own),
        grid=(4,),
        in_specs=[
            rows_block(length, half),
            rows_block(length, half),
            pl.BlockSpec((1,) + halo.shape[1:], lambda i: (i, 0, 0)),
            whole_block(taps.shape),
            whole_block(mix.shape),
        ],
        out_specs=[rows_block(length, columns) for columns, _ in shapes],
        out_shape=[jax.ShapeDtypeStruct((count, columns), kind) for columns, kind in shapes],
        compiler_params=params(),
        cost_estimate=pl.CostEstimate(
            flops=4 * count * half * half, bytes_accessed=16 * count * half, transcendentals=0
        ),
    )(c_part, product, halo, taps, mix)


def mix_back_kernel(
    half, own, d_ref, c_ref, conv_ref, p_ref, halo_ref, taps_ref, mix_ref, d_c_ref, d_p_ref, edge_ref, sums_ref
):
    grad = d_ref[...]
    d_gated = sum(
        times_transposed(
            grad[:, i * half : (i + 1) * half],
            flat(mix_ref[:, i * own // 4 : (i + 1) * own // 4, 3 * half :]),
        )
        for i in range(4)
    )
    d_c_ref[...] = narrow(d_gated * conv_ref[...])
    d_conv = d_gated * c_ref[...]
    product = wide(p_ref[...])
    one, two = delayed(product, wide(halo_ref[0]))

    @pl.when(pl.program_id(0) == 0)
    def _():
        sums_ref[...] = jnp.zeros_like(sums_ref)

    for k, value in enumerate((two, one, product)):
        sums_ref[k : k + 1] += jnp.sum(d_conv * value, axis=0, keepdims=True)
    taps = taps_ref[...]
    length = d_conv.shape[0]
    row = lax.broadcasted_iota(jnp.int32, d_conv.shape, 0)
    later = jnp.where(row < length - 1, pltpu.roll(d_conv, length - 1, 0), 0.0)
    latest = jnp.where(row < length - 2, pltpu.roll(d_conv, length - 2, 0), 0.0)
    d_p_ref[...] = taps[2:3] * d_conv + taps[1:2] * later + taps[0:1] * latest
    edge_ref[0, 0:1] = taps[0:1] * d_conv[0:1]
    edge_ref[0, 1:2] = taps[0:1] * d_conv[1:2] + taps[1:2] * d_conv[0:1]


def mix_back(d_branch, c_part, conv, product, halo, taps, mix, own):
    count, half = product.shape
    length = count // 4
    f32 = jnp.float32
    return pl.pallas_call(
        functools.partial(mix_back_kernel, half, own),
        grid=(4,),
        in_specs=[
            rows_block(length, 4 * half),
            rows_block(length, half),
            rows_block(length, half),
            rows_block(length, half),
            pl.BlockSpec((1,) + halo.shape[1:], lambda i: (i, 0, 0)),
            whole_block(taps.shape),
            whole_block(mix.shape),
        ],
        out_specs=[
            rows_block(length, half),
            rows_block(length, half),
            pl.BlockSpec((1, 2, half), lambda i: (i, 0, 0)),
            pl.BlockSpec((3, half), lambda i: (0, 0)),
        ],
        out_shape=[
            jax.ShapeDtypeStruct((count, half), jnp.bfloat16),
            jax.ShapeDtypeStruct((count, half), f32),
            jax.ShapeDtypeStruct((4, 2, half), f32),
            jax.ShapeDtypeStruct((3, half), f32),
        ],
        compiler_params=params(),
        cost_estimate=pl.CostEstimate(
            flops=4 * count * half * half // 10, bytes_accessed=2 * count * half, transcendentals=0
        ),
    )(d_branch, c_part, conv, product, halo, taps, mix)


def mix_last_kernel(
    half, own, d_p_ref, edge_ref, b_ref, x_ref, d_c_ref, tokens_ref, mix_ref, d_mixed_ref, d_n_ref, sums_ref
):
    d_product = d_p_ref[...]
    length = d_product.shape[0]
    row = lax.broadcasted_iota(jnp.int32, d_product.shape, 0)
    edge = edge_ref[0]
    d_product += jnp.where(
        row == length - 2, edge[0:1], jnp.where(row == length - 1, edge[1:2], 0.0)
    )
    d_mixed_ref[:, :half] = narrow(d_product * x_ref[...])
    d_mixed_ref[:, half : 2 * half] = d_c_ref[...]
    d_mixed_ref[:, 2 * half :] = narrow(d_product * b_ref[...])
    d_normed = times_transposed(d_mixed_ref[...], flat(mix_ref[:, :own, : 3 * half]))
    d_n_ref[...] = narrow(d_normed)
    inputs = wide(tokens_ref[...])
    unit = inputs * lax.rsqrt(jnp.mean(inputs * inputs, axis=-1, keepdims=True) + epsilon)

    @pl.when(pl.program_id(0) == 0)
    def _():
        sums_ref[...] = jnp.zeros_like(sums_ref)

    sums_ref[...] += jnp.sum(d_normed * unit, axis=0, keepdims=True)


def mix_last(d_product, edge, b_part, x_part, d_c, tokens, mix, own):
    count, half = d_product.shape
    length = count // 4
    return pl.pallas_call(
        functools.partial(mix_last_kernel, half, own),
        grid=(4,),
        in_specs=[
            rows_block(length, half),
            pl.BlockSpec((1, 2, half), lambda i: (i, 0, 0)),
            rows_block(length, half),
            rows_block(length, half),
            rows_block(length, half),
            rows_block(length, 4 * half),
            whole_block(mix.shape),
        ],
        out_specs=[
            rows_block(length, 3 * half),
            rows_block(length, 4 * half),
            pl.BlockSpec((1, 4 * half), lambda i: (0, 0)),
        ],
        out_shape=[
            jax.ShapeDtypeStruct((count, 3 * half), jnp.bfloat16),
            jax.ShapeDtypeStruct((count, 4 * half), jnp.bfloat16),
            jax.ShapeDtypeStruct((1, 4 * half), jnp.float32),
        ],
        compiler_params=params(),
        cost_estimate=pl.CostEstimate(
            flops=12 * count * half * half // 10, bytes_accessed=2 * count * half, transcendentals=0
        ),
    )(d_product, edge, b_part, x_part, d_c, tokens, mix)


def feed_forward_kernel(size, top, rows_ref, cot_ref, chunk_ref, *refs):
    hidden_ref, d_both_ref, d_rows_ref, out_ref = refs[-4:]
    rows = rows_ref[...]
    cot = cot_ref[...]
    down = flat(chunk_ref[:, 2 * top :, : rows.shape[1]])
    for start in range(0, size, 256):
        stop = min(start + 256, size)
        gate = times(rows, flat(chunk_ref[:, :top, start:stop]))
        upper = times(rows, flat(chunk_ref[:, top : 2 * top, start:stop]))
        d_hidden = times_transposed(cot, down[start:stop])
        sigma = jax.nn.sigmoid(gate)
        activated = gate * sigma
        hidden_ref[:, start:stop] = narrow(activated * upper)
        d_both_ref[:, start:stop] = narrow(d_hidden * upper * sigma * (1.0 + gate * (1.0 - sigma)))
        d_both_ref[:, size + start : size + stop] = narrow(d_hidden * activated)
    d_rows = times_transposed(d_both_ref[:, :size], flat(chunk_ref[:, :top]))
    d_rows += times_transposed(d_both_ref[:, size:], flat(chunk_ref[:, top : 2 * top]))
    d_rows_ref[...] = narrow(d_rows)
    out_ref[...] = narrow(times(hidden_ref[...], down))


def feed_forward(rows, cot, chunk, at, kept=(), first=()):
    width = rows.shape[1]
    tokens = cot.shape[0] // 2
    tile = tokens // 2
    size = chunk.shape[2]
    here = 2 * at
    aliases = {3 + i: i for i in range(len(kept))}
    return pl.pallas_call(
        functools.partial(feed_forward_kernel, size, width // chunk.shape[0]),
        grid=(2,),
        in_specs=[
            rows_block(tile, width, here if rows.shape[0] > tokens else 0),
            rows_block(tile, width, here),
            whole_block(chunk.shape),
        ]
        + [pl.BlockSpec(memory_space=pl.ANY)] * (len(kept) + len(first)),
        out_specs=[
            rows_block(tile, size, here),
            rows_block(tile, 2 * size, here),
            rows_block(tile, width),
            rows_block(tile, width),
        ],
        out_shape=[
            jax.ShapeDtypeStruct((2 * tokens, size), jnp.bfloat16),
            jax.ShapeDtypeStruct((2 * tokens, 2 * size), jnp.bfloat16),
            jax.ShapeDtypeStruct((tokens, width), jnp.bfloat16),
            jax.ShapeDtypeStruct((tokens, width), jnp.bfloat16),
        ],
        input_output_aliases=aliases,
        compiler_params=params(),
        cost_estimate=pl.CostEstimate(
            flops=12 * tokens * width * size,
            bytes_accessed=16 * tokens * width,
            transcendentals=tokens * size,
        ),
    )(rows, cot, chunk, *kept, *first)


def lay_out_kernel(groups, member_ref, parts_ref, gate_ref, up_ref, down_ref):
    member = member_ref[0]
    size = parts_ref.shape[2] // groups
    rows = gate_ref.shape[0]
    for place in range(4):
        part = wide(parts_ref[jnp.bitwise_xor(place, member)])
        for half, out_ref in enumerate((gate_ref, up_ref)):
            for group in range(groups):
                start = (group * 4 + place) * size
                out_ref[:, start : start + size] = part[
                    half * rows : (half + 1) * rows, group * size : (group + 1) * size
                ]
        down_ref[place * size : (place + 1) * size, :] = part[2 * rows :, : down_ref.shape[1]]


def lay_out(parts, member, groups, rows, width):
    columns = parts.shape[2]
    shapes = [(rows, 4 * columns), (rows, 4 * columns), (4 * columns // groups, width)]
    return pl.pallas_call(
        functools.partial(lay_out_kernel, groups),
        out_shape=[jax.ShapeDtypeStruct(shape, jnp.float32) for shape in shapes],
        in_specs=[
            pl.BlockSpec(memory_space=pltpu.SMEM),
            pl.BlockSpec(memory_space=pltpu.VMEM),
        ],
        out_specs=[pl.BlockSpec(memory_space=pltpu.VMEM)] * 3,
        compiler_params=params(),
        cost_estimate=pl.CostEstimate(
            flops=0, bytes_accessed=72 * rows * columns, transcendentals=0
        ),
    )(member[None], parts)


def lay_out_mix_kernel(groups, own, member_ref, parts_ref, in_ref, out_ref, small_ref):
    member = member_ref[0]
    part_size = parts_ref.shape[2] // 4
    lane = part_size // groups
    rows = own // 4
    for place in range(4):
        part = wide(parts_ref[jnp.bitwise_xor(place, member)])
        for group in range(3 * groups):
            start = (group * 4 + place) * lane
            in_ref[:, start : start + lane] = part[:own, group * lane : (group + 1) * lane]
        for i in range(4):
            out_ref[place * rows : (place + 1) * rows, i * part_size : (i + 1) * part_size] = part[
                i * rows : (i + 1) * rows, 3 * part_size :
            ]
    few = [wide(parts_ref[i])[own:, :own] for i in range(4)]
    small_ref[...] = (few[0] + few[1]) + (few[2] + few[3])


def lay_out_mix(parts, member, groups, own):
    width = parts.shape[2]
    shapes = [(own, 3 * width), (own, width), (parts.shape[1] - own, own)]
    return pl.pallas_call(
        functools.partial(lay_out_mix_kernel, groups, own),
        out_shape=[jax.ShapeDtypeStruct(shape, jnp.float32) for shape in shapes],
        in_specs=[
            pl.BlockSpec(memory_space=pltpu.SMEM),
            pl.BlockSpec(memory_space=pltpu.VMEM),
        ],
        out_specs=[pl.BlockSpec(memory_space=pltpu.VMEM)] * 3,
        compiler_params=params(),
        cost_estimate=pl.CostEstimate(flops=0, bytes_accessed=24 * own * width, transcendentals=0),
    )(member[None], parts)


def four_gather(value):
    across = over_y(value)
    return jnp.concatenate([value, over_core(value), across, over_core(across)], 0)


def far_sum(value):
    rows = value.shape[0] // 4
    return narrow(wide(over_core(value[3 * rows :])) + wide(value[2 * rows : 3 * rows]))


def near_sum(value):
    rows = value.shape[0] // 4
    return wide(value[:rows]) + wide(over_core(value[rows : 2 * rows]))


def picked(value, groups, parts, part, first=0, size=None):
    whole = value.shape[1] // (groups * parts)
    size = whole if size is None else size
    row = lax.broadcasted_iota(jnp.int32, (value.shape[1], groups * size), 0)
    column = lax.broadcasted_iota(jnp.int32, (value.shape[1], groups * size), 1)
    wanted = (column // size * parts + part) * whole + first + column % size
    return narrow(times(value, (row == wanted).astype(value.dtype)))


def local(
    tokens,
    cotangent,
    in_weight,
    out_weight,
    gate_weight,
    up_weight,
    down_weight,
    mix_gain,
    ffn_gain,
    conv_taps,
):
    shards = lax.axis_size("shard")
    core = lax.axis_index("core")
    member = lax.axis_index("y") * 2 + core
    width = tokens.shape[-1]
    length = tokens.shape[1]
    half = width // 4
    own = mix_gain.shape[0]
    lane = half // shards

    small = jnp.concatenate([mix_gain[None], ffn_gain[None], conv_taps], 0)
    in_mine = jnp.concatenate(
        [picked(in_weight[:, i * width : (i + 1) * width], shards, 4, member) for i in range(3)], 1
    )
    out_rows = own // 4
    out_mine = lax.dynamic_slice(out_weight, (member * out_rows, 0), (out_rows, width))
    out_mine = jnp.concatenate([out_mine[:, i * half : (i + 1) * half] for i in range(4)], 0)
    small_rows = jnp.pad(small, ((0, 11), (0, 4 * half - own)))
    mix_ring = Gather(
        jnp.concatenate([jnp.concatenate([in_mine, out_mine], 1), small_rows], 0), False
    )
    tokens_across = over_y(tokens[0])
    mix_ring.hop()

    quarter = down_weight.shape[0] // 4
    size = shards * quarter
    both = jnp.concatenate([gate_weight, up_weight], 0)
    if FIRST == 1:
        both = tie(both, mix_ring.one, mix_ring.two)
    both = picked(both, shards, 4, member)
    down = lax.dynamic_slice(down_weight, (member * quarter, 0), (quarter, width))
    block = jnp.concatenate([both, jnp.pad(down, ((0, 0), (0, size - width)))], 0)
    mix_ring.hop()
    mix_ring.one = tie(mix_ring.one, tokens_across)
    if FIRST == 2:
        block = tie(block, mix_ring.one, mix_ring.two)
    mix_ring.hop()
    if FIRST == 3:
        block = tie(block, mix_ring.one, mix_ring.two)
    mix = mix_ring.end()
    pair = jnp.concatenate(
        [tokens[0], over_core(tokens[0]), tokens_across, over_core(tokens_across)], 0
    )
    ring = Gather(block, True)
    ring.hop()
    ring.hop()

    small = wide(mix[:, own : own + 5, :own].transpose(1, 0, 2).reshape(5, width))
    gain_one, gain_two = small[0:1], small[1]
    taps = lax.dynamic_index_in_dim(
        small[2:5].reshape(3, shards, 4, lane), member, 2, keepdims=False
    ).reshape(3, half)

    normed, b_part, c_part, x_part, product = mix_in(pair, gain_one, mix, own)
    halo = lax.ppermute(
        product.reshape(4, length, half)[:, length - 2 :],
        "shard",
        [(i, i + 1) for i in range(shards - 1)],
    )
    conv, gated, branch = mix_out(c_part, product, halo, taps, mix, own)
    inputs = wide(tokens[0])
    resid = inputs + near_sum(branch) + wide(over_y(far_sum(branch)))

    factor_two = lax.rsqrt(jnp.mean(resid * resid, axis=-1, keepdims=True) + epsilon)
    unit_two = resid * factor_two
    hnorm = narrow(unit_two * gain_two)
    if AFTER:
        ring.one, ring.two = tie(ring.one, hnorm), tie(ring.two, hnorm)
    chunk = ring.end()
    if quarter % 16:
        chunk = jnp.concatenate(
            [flat(chunk[:, :own]), flat(chunk[:, own : 2 * own]), flat(chunk[:, 2 * own :])], 0
        )[None]
    across = over_y(hnorm)
    hnorm_near = jnp.concatenate([hnorm, over_core(hnorm)], 0)
    cot = cotangent[0]
    cot_across = over_y(cot)
    cot_all = jnp.concatenate([cot, over_core(cot), cot_across, over_core(cot_across)], 0)

    hidden, d_both, d_near, out_near = feed_forward(hnorm_near, cot_all, chunk, 0)
    across = tie(across, hidden)
    hnorm_all = jnp.concatenate([hnorm_near, across, over_core(across)], 0)
    hidden, d_both, d_far, out_far = feed_forward(hnorm_all, cot_all, chunk, 1, (hidden, d_both))
    g_down = outer_sum(hidden, cot_all)
    d_far = narrow(wide(over_core(d_far[length:])) + wide(d_far[:length]))
    d_both = tie(d_both, d_far)
    d_far = over_y(d_far)
    g_both = outer_sum(hnorm_all, d_both)

    def part(place):
        both = lax.dynamic_slice(g_both, (place * own, 0), (own, 2 * size))
        down = lax.dynamic_slice(g_down, (place * quarter, 0), (quarter, width))
        down = jnp.pad(down, ((0, 0), (0, size - width)))
        return jnp.concatenate([both[:, :size], both[:, size:], down], 0)

    back = Scatter(part, True)
    back.hop()
    d_near = wide(d_near[:length]) + wide(over_core(d_near[length:]))
    d_hnorm = d_near + wide(d_far)

    g_ffn_gain = jnp.sum(d_hnorm * unit_two, axis=0, keepdims=True)
    scaled_two = d_hnorm * gain_two
    d_resid = wide(cotangent[0]) + factor_two * (
        scaled_two - unit_two * jnp.mean(scaled_two * unit_two, axis=-1, keepdims=True)
    )
    d_own = narrow(d_resid)
    back.one, back.two = tie(back.one, d_own), tie(back.two, d_own)
    back.hop()
    d_branch = four_gather(d_own)
    back.one, back.two = tie(back.one, d_branch), tie(back.two, d_branch)
    back.hop()
    d_c, d_product, edge, tap_grads = mix_back(
        d_branch, c_part, conv, product, halo, taps, mix, own
    )
    returned = lax.ppermute(edge, "shard", [(i + 1, i) for i in range(shards - 1)])
    g_out = outer_sum(gated, d_branch)
    d_mixed, d_normed, g_mix_gain = mix_last(
        d_product, returned, b_part, x_part, d_c, pair, mix, own
    )
    g_in = outer_sum(normed, d_mixed)
    spot = lax.broadcasted_iota(jnp.int32, (3, shards, 4, lane), 2)
    tap_full = jnp.where(spot == member, tap_grads.reshape(3, shards, 1, lane), 0.0)
    small_grads = jnp.concatenate([g_mix_gain, g_ffn_gain, tap_full.reshape(3, width)], 0)

    def mix_part(place):
        out = lax.dynamic_slice(g_out, (place * out_rows, 0), (out_rows, width))
        out = jnp.concatenate([out[:, i * half : (i + 1) * half] for i in range(4)], 0)
        main = lax.dynamic_slice(g_in, (place * own, 0), (own, 3 * half))
        few = lax.dynamic_slice(small_grads, (0, place * own), (5, own))
        few = jnp.pad(few, ((0, 11), (0, 4 * half - own)))
        return jnp.concatenate([jnp.concatenate([main, out], 1), few], 0)

    back_mix = Scatter(mix_part, False)
    third = (back.one, back.two)
    back.hop()
    back_mix.hop()
    out_far = narrow(wide(over_core(out_far[length:])) + wide(out_far[:length]))
    out_far = over_y(tie(out_far, d_far))
    out_near = wide(out_near[:length]) + wide(over_core(out_near[length:]))
    if BACK == 1:
        back_mix.one = tie(back_mix.one, out_far, *third)
    if BACK == 2:
        back_mix.one = tie(back_mix.one, out_far, back.one)
    back_mix.hop()
    output = narrow(tie(resid, back_mix.one) + out_near + wide(out_far))
    d_normed_far = over_y(tie(far_sum(d_normed), out_far))
    back_mix.one = tie(back_mix.one, d_normed_far)
    d_normed = near_sum(d_normed) + wide(d_normed_far)
    factor_one = lax.rsqrt(jnp.mean(inputs * inputs, axis=-1, keepdims=True) + epsilon)
    unit_one = inputs * factor_one
    scaled_one = d_normed * gain_one
    d_inputs = d_resid + factor_one * (
        scaled_one - unit_one * jnp.mean(scaled_one * unit_one, axis=-1, keepdims=True)
    )

    def summed(value):
        return narrow(lax.psum(value, "outer") if lax.axis_size("outer") > 1 else value)

    def four_parts(value):
        mine = summed(value)
        across = over_y(mine)
        return jnp.stack([mine, over_core(mine), across, over_core(across)], 0)

    owned_gate, owned_up, owned_down = lay_out(
        four_parts(back.end()), member, shards, own, width
    )

    owned_in, owned_out, small_owned = lay_out_mix(
        four_parts(back_mix.end()), member, shards, own
    )
    return (
        output[None],
        narrow(d_inputs)[None],
        owned_in,
        owned_out,
        owned_gate,
        owned_up,
        owned_down,
        small_owned[0],
        small_owned[1],
        small_owned[2:5],
    )


def solution(mesh):
    shards = mesh.shape["shard"]
    reps = mesh.shape["rep"]
    finer = Mesh(mesh.devices.reshape(shards, reps // 4, 2, 2), ("shard", "outer", "y", "core"))
    rep = ("outer", "y", "core")
    specs = (
        P(rep, "shard", None),
        P(rep, "shard", None),
        P("shard", None),
        P("shard", None),
        P("shard", None),
        P("shard", None),
        P("shard", None),
        P("shard"),
        P("shard"),
        P(None, "shard"),
    )
    return jax.shard_map(local, mesh=finer, in_specs=specs, out_specs=specs, check_vma=False)
```
